256 devices in a mesh: wide: 32 (over x, y, core), narrow: 8 (over z).
Axes of the slice: x: 4, y: 4, z: 8, core: 2. Of those that a mesh axis runs over, the one named last changes fastest.
Arguments:
- activity: bfloat16 [256, 8, 512, 512], P(('wide', 'narrow')), may hold values from 0 to 1
- tile_coords: int32 [256, 2], replicated, may hold values from 0 to 31, as said below
- user_owner: int32 [32], replicated, may hold values from 0 to 31, each once
- item_owner: int32 [32], replicated, may hold values from 0 to 31, each once
- user_factor: float32 [16384, 256], P('wide', 'narrow'), may hold values from 0 to 1
- item_factor: float32 [16384, 256], P('wide', 'narrow'), may hold values from 0 to 1
- time_factor: float32 [8, 256], replicated, may hold values from 0.0003 to 0.003
- user_dual: float32 [16384, 256], P('wide', 'narrow'), may hold values from -1.8 to 1.8
- item_dual: float32 [16384, 256], P('wide', 'narrow'), may hold values from -1.8 to 1.8
Outputs:
- new_users: float32 [16384, 256], P('wide', 'narrow')
- new_items: float32 [16384, 256], P('wide', 'narrow')
- new_user_dual: float32 [16384, 256], P('wide', 'narrow')
- new_item_dual: float32 [16384, 256], P('wide', 'narrow')
The draws below stay inside these ranges and needn't reach their ends.
Inputs may be any that keep to these rules, and one draw needn't show every extreme that they name: `tile_coords`: no pair of blocks appears twice. `user_owner`: each stored row block holds exactly one user block. `item_owner`: each stored row block holds exactly one item block.
All inputs are finite; a program needn't handle non-finite values.
Results may differ from the reference program's by a relative error of at most 0.0017.
The reference program's roundings to bfloat16 on the way count: a program that leaves them out, or rounds other values in their place, can miss the bound.
Values may be sent and summed in bfloat16 or wider, within the bound.
A program may use at most 64 MiB of HBM per device.

```python
import math
import jax
import jax.numpy as jnp
from jax import lax

RANK = 256
BLOCK = 512
TIMES = 8
PASSES = 2
BLOCKS = 32
TILES = 256


def draw_tile_coords(key, part):
    chosen = jax.random.permutation(jax.random.fold_in(key, 11), BLOCKS * BLOCKS)[:TILES]
    return jnp.stack([chosen // BLOCKS, chosen % BLOCKS], axis=1).astype(jnp.int32)


def block_levels(rng, dims, cuts, smallest, high):
    level, own = 1.0, jax.random.fold_in(rng, 6)
    for dim, blocks in cuts:
        heights = jnp.exp(jax.random.uniform(jax.random.fold_in(own, dim), (blocks,), jnp.float32, smallest / len(cuts), high / len(cuts)))
        level = level * jnp.repeat(heights, dims[dim] // blocks).reshape([-1 if axis == dim else 1 for axis in range(len(dims))])
    return level


def bell_draw(key, shape, width, bound, split=(), kind=jnp.bfloat16):
    entries = width * jax.random.normal(key, shape, jnp.float32)
    if split:
        entries = entries * block_levels(key, shape, split, -0.22, 0.18)
    return jnp.clip(entries, -bound, bound).astype(kind)


def setup_inputs(seed: int = 0) -> dict:
    streams_of = jax.random.split(jax.random.key(seed), 10)
    return {
        "activity": jnp.clip(1.0 * jax.random.uniform(streams_of[0], (TILES, TIMES, BLOCK, BLOCK), jnp.float32) ** block_levels(streams_of[0], (TILES, TIMES, BLOCK, BLOCK), ((0, 256),), -0.2, 0.2), 0.0, 1.0).astype(jnp.bfloat16),
        "tile_coords": draw_tile_coords(jax.random.fold_in(streams_of[9], 71), 0),
        "user_owner": jax.random.permutation(streams_of[2], BLOCKS).astype(jnp.int32),
        "item_owner": jax.random.permutation(streams_of[3], BLOCKS).astype(jnp.int32),
        "user_factor": jnp.clip(1.0 * jax.random.uniform(streams_of[4], (BLOCKS * BLOCK, RANK), jnp.float32) ** block_levels(streams_of[4], (BLOCKS * BLOCK, RANK), ((0, 32), (1, 8)), -0.2, 0.2), 0.0, 1.0),
        "item_factor": jnp.clip(1.0 * jax.random.uniform(streams_of[5], (BLOCKS * BLOCK, RANK), jnp.float32) ** block_levels(streams_of[5], (BLOCKS * BLOCK, RANK), ((0, 32), (1, 8)), -0.2, 0.2), 0.0, 1.0),
        "time_factor": jnp.clip(jnp.exp(jax.random.uniform(streams_of[6], (TIMES, RANK), jnp.float32, math.log(0.0003), math.log(0.003))), 0.0003, 0.003),
        "user_dual": bell_draw(streams_of[7], (BLOCKS * BLOCK, RANK), 0.3, 1.8, ((0, 32), (1, 8)), jnp.float32),
        "item_dual": bell_draw(streams_of[8], (BLOCKS * BLOCK, RANK), 0.3, 1.8, ((0, 32), (1, 8)), jnp.float32),
    }


def sums_for(activity, other, time_factor, own_pos, other_pos, forward):
    lowered = other.astype(jnp.bfloat16).reshape(BLOCKS, BLOCK, RANK)

    def add_tile(total, inputs):
        tile, own_block, other_block = inputs
        picked = lax.dynamic_index_in_dim(lowered, other_block, 0, keepdims=False)
        khatri = (picked.astype(jnp.float32)[None] * time_factor[:, None, :]).astype(jnp.bfloat16)
        tile_wide = tile.astype(jnp.float32)
        khatri_wide = khatri.astype(jnp.float32)
        if forward:
            partial_value = jnp.einsum('kij,kjr->ir', tile_wide, khatri_wide, precision=lax.Precision.HIGHEST)
        else:
            partial_value = jnp.einsum('kij,kir->jr', tile_wide, khatri_wide, precision=lax.Precision.HIGHEST)
        return (total.at[own_block].add(partial_value), None)
    start = jnp.zeros((BLOCKS, BLOCK, RANK), jnp.float32)
    total, _ = lax.scan(add_tile, start, (activity, own_pos, other_pos))
    return total.reshape(BLOCKS * BLOCK, RANK)

def admm_update(sums, factor, dual, other, time_factor):
    gram = jnp.dot(other.T, other, precision=lax.Precision.HIGHEST)
    gram = gram * jnp.dot(time_factor.T, time_factor, precision=lax.Precision.HIGHEST)
    penalty = jnp.trace(gram) / RANK
    identity = jnp.eye(RANK, dtype=jnp.float32)
    lower = jnp.linalg.cholesky(gram + penalty * identity)
    inverse = jax.scipy.linalg.cho_solve((lower, True), identity)
    for _ in range(PASSES):
        target = jnp.dot(sums + penalty * (factor + dual), inverse, precision=lax.Precision.HIGHEST)
        factor = jnp.maximum(target - dual, 0.0)
        dual = dual + factor - target
    return (factor, dual)

def reference(activity, tile_coords, user_owner, item_owner, user_factor, item_factor, time_factor, user_dual, item_dual):
    user_pos = user_owner[tile_coords[:, 0]].astype(jnp.int32)
    item_pos = item_owner[tile_coords[:, 1]].astype(jnp.int32)
    user_sums = sums_for(activity, item_factor, time_factor, user_pos, item_pos, True)
    new_users, new_user_dual = admm_update(user_sums, user_factor, user_dual, item_factor, time_factor)
    item_sums = sums_for(activity, new_users, time_factor, item_pos, user_pos, False)
    new_items, new_item_dual = admm_update(item_sums, item_factor, item_dual, new_users, time_factor)
    return (new_users, new_items, new_user_dual, new_item_dual)
```

```python
import jax
import jax.numpy as jnp
from jax import lax
from jax.experimental import pallas as pl
from jax.experimental.pallas import tpu as pltpu
from jax.sharding import Mesh
from jax.sharding import PartitionSpec as P

RANK = 256
BLOCK = 512
TIMES = 8
PASSES = 2
SIDE = 4
CORES = 2
DEPTH = 8
STEPS = 7
MESH = pl.DeviceIdType.MESH
WIDE = ("wide_0", "wide_1", "wide_2")
WIDE_NARROW = ("wide_0", "wide_1", "wide_2", "narrow")
SEMS = 440
F32 = jnp.float32
BF16 = jnp.bfloat16


def exact_dot(a, b):
    return jnp.dot(a, b, precision=lax.Precision.HIGHEST, preferred_element_type=F32)


def sweep_kernel(
    act_hbm,
    coords,
    user_owner,
    item_owner,
    user_factor,
    item_factor,
    time_factor,
    user_dual,
    item_dual,
    out_users,
    out_items,
    out_user_dual,
    out_item_dual,
    act,
    packed,
    landed,
    held,
    khatri,
    gath,
    zsend,
    kbuf,
    gpart,
    fix,
    fix_land,
    gland,
    gfull,
    base,
    approx,
    partial,
    tland,
    cland,
    dense,
    first_land,
    middle,
    last_land,
    opack,
    oland,
    sems,
    act_sem,
):
    x, y, c, z = (lax.axis_index(name) for name in WIDE_NARROW)
    wide = (x * SIDE + y) * CORES + c
    twin = (x * SIDE + y) * CORES + (1 - c)
    twin_dev = (x, y, 1 - c, z)

    def x_dev(d):
        return (lax.rem(x + d, SIDE), y, c, z)

    def y_dev(d):
        return (x, lax.rem(y + d, SIDE), c, z)

    def z_at(d):
        return lax.rem(z + d, DEPTH)

    def z_dev(d):
        return (x, y, c, z_at(d))

    around = (4, 3, 5, 2, 6, 1, 7)

    load_act = pltpu.make_async_copy(act_hbm.at[0], act, act_sem)
    load_act.start()

    barrier = pltpu.get_barrier_semaphore()
    peers = [x_dev(d) for d in (1, 2, 3)] + [y_dev(d) for d in (1, 2, 3)]
    peers += [z_dev(d) for d in range(1, DEPTH)] + [twin_dev]
    for peer in peers:
        pl.semaphore_signal(barrier, inc=1, device_id=peer, device_id_type=MESH)

    count = [0]
    sent = []

    def send(src, dst, device):
        k = count[0]
        count[0] += 2
        assert count[0] <= SEMS
        copy = pltpu.make_async_remote_copy(
            src_ref=src,
            dst_ref=dst,
            send_sem=sems.at[k],
            recv_sem=sems.at[k + 1],
            device_id=device,
            device_id_type=MESH,
        )
        copy.start()
        sent.append(copy)
        return copy

    def pack(which, ref):
        stacked = jnp.concatenate([ref[:, t * 128 : (t + 1) * 128] for t in range(4)], axis=0)
        packed[which] = stacked.T

    def lines(place, size):
        return pl.ds(pl.multiple_of(place * size, size), size)

    def unpack(which):
        for t in range(4):
            held[which, t * 16 : (t + 1) * 16] = jnp.concatenate(
                [landed[which, n, :, t * 32 : (t + 1) * 32] for n in range(DEPTH)], axis=1
            )

    pack(0, item_factor)
    pl.semaphore_wait(barrier, len(peers))
    lead = [
        send(packed.at[0, lines(z_at(d), 16)], landed.at[0, z], z_dev(d)) for d in around
    ]
    landed[0, z] = packed[0, lines(z, 16)]
    pack(1, item_dual)
    pack(2, user_factor)
    pack(3, user_dual)
    rest = [
        send(packed.at[pl.ds(1, 3), lines(z_at(d), 16)], landed.at[pl.ds(1, 3), z], z_dev(d))
        for d in around
    ]
    for a in (1, 2, 3):
        landed[a, z] = packed[a, lines(z, 16)]
    times = time_factor[...]
    time_gram = exact_dot(times.T, times)
    eye = (
        lax.broadcasted_iota(jnp.int32, (RANK, RANK), 0)
        == lax.broadcasted_iota(jnp.int32, (RANK, RANK), 1)
    ).astype(F32)
    for copy in lead:
        copy.wait_recv()
    unpack(0)

    def unpack_rest():
        for copy in rest:
            copy.wait_recv()
        for a in (1, 2, 3):
            unpack(a)

    def gather(p, rows, after_start, after_middle):
        buf = gath.at[p]
        for h in range(2):
            buf[h, x, y, c] = rows[h * 32 : (h + 1) * 32].astype(BF16)
        starts = [
            send(buf.at[h, x, y, c], buf.at[h, x, y, c], (x_dev, y_dev)[h](d))
            for d in (2, 1, 3)
            for h in range(2)
        ]
        high = rows.astype(BF16)
        low = rows - high.astype(F32)
        missed = lax.dot_general(
            (high.astype(F32) + 0.5 * low).astype(BF16),
            low.astype(BF16),
            (((0,), (0,)), ((), ())),
            preferred_element_type=F32,
        )
        fix[p, 0:RANK] = (missed + missed.T).astype(BF16)
        fixes = [
            send(fix.at[p, lines(lax.rem(x + d, SIDE), 64)], fix_land.at[p, d - 1, 0:64], x_dev(d))
            for d in (2, 1, 3)
        ]
        after_start()
        for copy in starts:
            copy.wait_recv()
        mine = (buf.at[0, :, y, c], buf.at[1, x, :, c])
        middles = [
            (h, d, send(mine[h], mine[h], (y_dev, x_dev)[h](d)))
            for d in (2, 1, 3)
            for h in range(2)
        ]
        twins = [send(mine[h], mine[h], twin_dev) for h in range(2)]
        for copy in fixes:
            copy.wait_recv()
        total = fix[p, lines(x, 64)].astype(F32)
        for d in (1, 2, 3):
            total += fix_land[p, d - 1, 0:64].astype(F32)
        fix[p, RANK : RANK + 64] = total.astype(BF16)
        fixes = [
            send(
                fix.at[p, lines(lax.rem(y + d, SIDE) + 16, 16)],
                fix_land.at[p, d - 1, 64:80],
                y_dev(d),
            )
            for d in (2, 1, 3)
        ]
        after_middle()
        for h, d, copy in sorted(middles, key=lambda entry: (entry[1] + 1) % 4):
            copy.wait_recv()
            if h == 0:
                part = buf.at[0, :, lax.rem(y + SIDE - d, SIDE), c]
            else:
                part = buf.at[1, lax.rem(x + SIDE - d, SIDE), :, c]
            twins.append(send(part, part, twin_dev))
        for copy in fixes:
            copy.wait_recv()
        total = fix[p, lines(y + 16, 16)].astype(F32)
        for d in (1, 2, 3):
            total += fix_land[p, d - 1, 64:80].astype(F32)
        fix[p, RANK + 64 : RANK + 80] = total.astype(BF16)
        twins.append(
            send(fix.at[p, RANK + 64 : RANK + 80], fix_land.at[p, 0, 80:96], twin_dev)
        )
        for copy in twins:
            copy.wait_recv()

    def fetch(p, coord, owner):
        def choose(j):
            place = owner[coords[coord, wide * DEPTH + j]]
            spot = (place // 8, (place // 2) % SIDE, place % CORES)
            for h in range(2):
                zsend[p, j, 2 * h : 2 * h + 2] = gath[p, h, spot[0], spot[1], spot[2]].reshape(
                    2, 16, RANK
                )

        copies = []
        for d in around:
            choose(z_at(d))
            copies.append(send(zsend.at[p, z_at(d)], kbuf.at[p, :, z], z_dev(d)))
        choose(z)
        kbuf[p, :, z] = zsend[p, z]
        return copies

    def gram_start(p):
        total = jnp.zeros((RANK, RANK), F32)
        for h in range(2):
            for a in range(SIDE):
                some = gath[p, h, a].reshape(SIDE * CORES * 32, RANK)
                total += lax.dot_general(
                    some, some, (((0,), (0,)), ((), ())), preferred_element_type=F32
                )
        gpart[p] = total
        own = lines(wide, 8)
        both = fix[p, RANK + 64 : RANK + 80].astype(F32) + fix_land[p, 0, 80:96].astype(F32)
        gpart[p, own] += jnp.where(c == 0, both[0:8], both[8:16])
        copies = [send(gpart.at[p, own], gland.at[p, z], z_dev(d)) for d in around]
        gland[p, z] = gpart[p, own]
        for copy in copies:
            copy.wait_recv()
        gfull[p, x, y, c] = jnp.sum(gland[p], axis=0)
        spot = gfull.at[p, x, y, c]
        copies = [send(spot, spot, x_dev(d)) for d in (2, 1, 3)]
        for copy in copies:
            copy.wait_recv()
        line = gfull.at[p, :, y, c]
        return [send(line, line, y_dev(d)) for d in (2, 1, 3)]

    def gram_end(p, copies):
        for copy in copies:
            copy.wait_recv()
        plane = gfull.at[p, :, :, c]
        send(plane, plane, twin_dev).wait_recv()
        gram = gfull[p].reshape(RANK, RANK) * time_gram
        penalty = jnp.sum(gram * eye) / RANK
        base[...] = gram / penalty + eye
        t = 129.0 / 128.0
        t2 = 2.0 * t * t - 1.0
        approx[...] = (eye * 2.0 - base[...] * (1.0 / 129.0)) * ((t2 + 1.0) / t2 / 129.0)

        def step(_, t):
            t2 = 2.0 * t * t - 1.0
            now = approx[...]
            rest = eye - exact_dot(base[...], now)
            approx[...] = (now + exact_dot(now, rest)) * ((t2 + 1.0) / t2)
            return t2

        lax.fori_loop(0, STEPS, step, F32(t2))
        return penalty

    def tile_half(p, h, forward, khatri_t):
        total = jnp.zeros((BLOCK // 2, RANK), F32)
        cut = slice(h * 256, (h + 1) * 256)
        for k in range(TIMES):
            if forward:
                total += jnp.dot(act[k, cut, :], khatri[k], preferred_element_type=F32)
            else:
                total += jnp.dot(khatri_t[k], act[k, :, cut], preferred_element_type=F32)
        if not forward:
            total = total.T
        partial[p, 2 * h : 2 * h + 2] = total.reshape(2, DEPTH, 16, RANK)
        pair = pl.ds(2 * h, 2)
        copies = [
            (d, send(partial.at[p, pair, z_at(d)], tland.at[p, h, z], z_dev(d))) for d in around
        ]
        tland[p, h, z] = partial[p, 2 * h : 2 * h + 2, z]
        return copies

    def reduced(p, coord, owner, copies):
        twins = [[], []]
        for h in range(2):
            spot = tland.at[p, h, z]
            twins[h].append(send(spot, cland.at[p, h, z], twin_dev))
            for d, copy in copies[h]:
                copy.wait_recv()
                origin = lax.rem(z + DEPTH - d, DEPTH)
                twins[h].append(send(tland.at[p, h, origin], cland.at[p, h, origin], twin_dev))
        targets = [owner[coords[coord, wide * DEPTH + j]] for j in range(DEPTH)]
        twin_targets = [owner[coords[coord, twin * DEPTH + j]] for j in range(DEPTH)]
        firsts = []
        for h in range(2):
            for copy in twins[h]:
                copy.wait_recv()

            def place(i, carry):
                a, b = i // SIDE, i % SIDE
                block = ((a * SIDE + b) if h == 0 else (b * SIDE + a)) * CORES + c
                total = jnp.zeros((2, 16, RANK), F32)
                for j in range(DEPTH):
                    total += tland[p, h, j] * (targets[j] == block).astype(F32)
                    total += cland[p, h, j] * (twin_targets[j] == block).astype(F32)
                dense[p, h, a, b] = total
                return carry

            lax.fori_loop(0, SIDE * SIDE, place, 0)
            me = (x, y)[h]
            for d in (2, 1, 3):
                firsts.append(
                    send(
                        dense.at[p, h, lax.rem(me + d, SIDE)],
                        first_land.at[p, h, d - 1],
                        (x_dev, y_dev)[h](d),
                    )
                )
        seconds = []
        for h in range(2):
            for copy in firsts[3 * h : 3 * h + 3]:
                copy.wait_recv()
            middle[p, h] = (dense[p, h, (x, y)[h]] + first_land[p, h, 0]) + (
                first_land[p, h, 1] + first_land[p, h, 2]
            )
            other = (y, x)[h]
            for d in (2, 1, 3):
                seconds.append(
                    send(
                        middle.at[p, h, lax.rem(other + d, SIDE)],
                        last_land.at[p, h, d - 1],
                        (y_dev, x_dev)[h](d),
                    )
                )
        halves = []
        for h in range(2):
            for copy in seconds[3 * h : 3 * h + 3]:
                copy.wait_recv()
            total = (middle[p, h, (y, x)[h]] + last_land[p, h, 0]) + (
                last_land[p, h, 1] + last_land[p, h, 2]
            )
            halves.append(total.reshape(32, RANK))
        return jnp.concatenate(halves, axis=0)

    def admm(sums, factor, dual, penalty):
        inverse = approx[...]
        for _ in range(PASSES):
            target = exact_dot(sums + penalty * (factor + dual), inverse) / penalty
            factor = jnp.maximum(target - dual, 0.0)
            dual = dual + factor - target
        return factor, dual

    def give_back(p, factor, dual):
        for a, rows in ((0, factor), (1, dual)):
            for n in range(DEPTH):
                opack[p, n, a] = jnp.concatenate(
                    [
                        rows[t * 16 : (t + 1) * 16, n * 32 : (n + 1) * 32]
                        for t in range(4)
                    ],
                    axis=1,
                )
        copies = [send(opack.at[p, z_at(d)], oland.at[p, :, z], z_dev(d)) for d in around]
        oland[p, :, z] = opack[p, z]
        return copies

    def take_back(p, copies, outs):
        for copy in copies:
            copy.wait_recv()
        for a in range(2):
            turned = oland[p, a].reshape(128, 128).T
            for t in range(4):
                outs[a][:, t * 128 : (t + 1) * 128] = turned[t * 32 : (t + 1) * 32, :]

    def update(p, rows, factor_at, dual_at, own_coord, own, other, after_start, after_middle, after_gram):
        forward = p == 0
        gather(p, rows, after_start, after_middle)
        fetched = fetch(p, 1 - own_coord, other)
        gram_copies = gram_start(p)
        after_gram()
        for copy in fetched:
            copy.wait_recv()
        if forward:
            load_act.wait()
        low = kbuf[p].reshape(BLOCK, RANK).astype(F32)
        khatri_t = None
        if forward:
            for k in range(TIMES):
                khatri[k] = (low * times[k : k + 1, :]).astype(BF16)
        else:
            turned = low.T
            columns = times.T
            khatri_t = [(turned * columns[:, k : k + 1]).astype(BF16) for k in range(TIMES)]
        copies = [tile_half(p, h, forward, khatri_t) for h in range(2)]
        penalty = gram_end(p, gram_copies)
        sums = reduced(p, own_coord, own, copies)
        return admm(sums, held[factor_at], held[dual_at], penalty)

    nothing = lambda: None
    users, user_duals = update(
        0, held[0], 2, 3, 0, user_owner, item_owner, nothing, unpack_rest, nothing
    )
    returned = []
    items, item_duals = update(
        1,
        users,
        0,
        1,
        1,
        item_owner,
        user_owner,
        lambda: returned.extend(give_back(0, users, user_duals)),
        nothing,
        lambda: take_back(0, returned, (out_users, out_user_dual)),
    )
    take_back(1, give_back(1, items, item_duals), (out_items, out_item_dual))
    for copy in sent:
        copy.wait_send()


def local(
    activity,
    tile_coords,
    user_owner,
    item_owner,
    user_factor,
    item_factor,
    time_factor,
    user_dual,
    item_dual,
):
    vmem = pl.BlockSpec(memory_space=pltpu.VMEM)
    smem = pl.BlockSpec(memory_space=pltpu.SMEM)
    slab = jax.ShapeDtypeStruct((RANK // DEPTH, BLOCK), F32)
    outs = pl.pallas_call(
        sweep_kernel,
        out_shape=(slab,) * 4,
        in_specs=[pl.BlockSpec(memory_space=pl.ANY), smem, smem, smem] + [vmem] * 5,
        out_specs=(vmem,) * 4,
        scratch_shapes=[
            pltpu.VMEM((TIMES, BLOCK, BLOCK), BF16),
            pltpu.VMEM((4, 128, 128), F32),
            pltpu.VMEM((4, DEPTH, 16, 128), F32),
            pltpu.VMEM((4, 64, RANK), F32),
            pltpu.VMEM((TIMES, BLOCK, RANK), BF16),
            pltpu.VMEM((2, 2, SIDE, SIDE, CORES, 32, RANK), BF16),
            pltpu.VMEM((2, DEPTH, 4, 16, RANK), BF16),
            pltpu.VMEM((2, 4, DEPTH, 16, RANK), BF16),
            pltpu.VMEM((2, RANK, RANK), F32),
            pltpu.VMEM((2, RANK + 80, RANK), BF16),
            pltpu.VMEM((2, SIDE - 1, 96, RANK), BF16),
            pltpu.VMEM((2, DEPTH, 8, RANK), F32),
            pltpu.VMEM((2, SIDE, SIDE, CORES, 8, RANK), F32),
            pltpu.VMEM((RANK, RANK), F32),
            pltpu.VMEM((RANK, RANK), F32),
            pltpu.VMEM((2, 4, DEPTH, 16, RANK), F32),
            pltpu.VMEM((2, 2, DEPTH, 2, 16, RANK), F32),
            pltpu.VMEM((2, 2, DEPTH, 2, 16, RANK), F32),
            pltpu.VMEM((2, 2, SIDE, SIDE, 2, 16, RANK), F32),
            pltpu.VMEM((2, 2, SIDE - 1, SIDE, 2, 16, RANK), F32),
            pltpu.VMEM((2, 2, SIDE, 2, 16, RANK), F32),
            pltpu.VMEM((2, 2, SIDE - 1, 2, 16, RANK), F32),
            pltpu.VMEM((2, DEPTH, 2, 16, 128), F32),
            pltpu.VMEM((2, 2, DEPTH, 16, 128), F32),
            pltpu.SemaphoreType.DMA((SEMS,)),
            pltpu.SemaphoreType.DMA,
        ],
        compiler_params=pltpu.CompilerParams(
            collective_id=0, has_side_effects=True, vmem_limit_bytes=48 * 2**20
        ),
        name="sweep",
    )(
        activity,
        tile_coords.T,
        user_owner,
        item_owner,
        user_factor.T,
        item_factor.T,
        time_factor,
        user_dual.T,
        item_dual.T,
    )
    users, items, user_duals, item_duals = (out.T for out in outs)
    return (users, items, user_duals, item_duals)


def solution(mesh):
    split = Mesh(
        mesh.devices.reshape(SIDE, SIDE, CORES, mesh.shape["narrow"]),
        WIDE_NARROW,
    )
    in_specs = (
        P(WIDE_NARROW, None, None, None),
        P(),
        P(),
        P(),
        P(WIDE, "narrow"),
        P(WIDE, "narrow"),
        P(),
        P(WIDE, "narrow"),
        P(WIDE, "narrow"),
    )
    out_specs = (P(WIDE, "narrow"), P(WIDE, "narrow"), P(WIDE, "narrow"), P(WIDE, "narrow"))
    return jax.shard_map(local, mesh=split, in_specs=in_specs, out_specs=out_specs, check_vma=False)
```

```python
import jax
import jax.numpy as jnp
from jax import lax
from jax.experimental import pallas as pl
from jax.experimental.pallas import tpu as pltpu
from jax.sharding import Mesh
from jax.sharding import PartitionSpec as P

RANK = 256
BLOCK = 512
TIMES = 8
PASSES = 2
SIDE = 4
CORES = 2
DEPTH = 8
STEPS = 7
SCALES = [129.0 / 128.0]
for _ in range(STEPS):
    SCALES.append(2.0 * SCALES[-1] ** 2 - 1.0)
MESH = pl.DeviceIdType.MESH
WIDE = ("wide_0", "wide_1", "wide_2")
WIDE_NARROW = ("wide_0", "wide_1", "wide_2", "narrow")
SEMS = 104
F32 = jnp.float32
BF16 = jnp.bfloat16


def exact_dot(a, b):
    return jnp.dot(a, b, precision=lax.Precision.HIGHEST, preferred_element_type=F32)


def sweep_kernel(
    act_hbm,
    coords_hbm,
    user_owner_hbm,
    item_owner_hbm,
    user_factor_hbm,
    item_factor_hbm,
    time_factor_hbm,
    user_dual_hbm,
    item_dual_hbm,
    out_users,
    out_items,
    out_user_duals,
    out_item_duals,
    act,
    coords,
    user_owner,
    item_owner,
    slabs,
    time_factor,
    packed,
    landed,
    held,
    khatri,
    gath,
    zsend,
    kbuf,
    gpart,
    fix,
    fix_land,
    gland,
    gfull,
    base,
    approx,
    partial,
    tland,
    cland,
    dense,
    first_land,
    middle,
    last_land,
    opack,
    oland,
    sems,
    load_sems,
):
    x, y, c, z = (lax.axis_index(name) for name in WIDE_NARROW)
    wide = (x * SIDE + y) * CORES + c
    twin = (x * SIDE + y) * CORES + (1 - c)
    twin_dev = (x, y, 1 - c, z)

    def x_dev(d):
        return (lax.rem(x + d, SIDE), y, c, z)

    def y_dev(d):
        return (x, lax.rem(y + d, SIDE), c, z)

    def z_at(d):
        return lax.rem(z + d, DEPTH)

    def z_dev(d):
        return (x, y, c, z_at(d))

    around = (4, 3, 5, 2, 6, 1, 7)

    barrier = pltpu.get_barrier_semaphore()
    peers = [x_dev(d) for d in (1, 2, 3)] + [y_dev(d) for d in (1, 2, 3)]
    peers += [z_dev(d) for d in range(1, DEPTH)] + [twin_dev]
    for peer in peers:
        pl.semaphore_signal(barrier, inc=1, device_id=peer, device_id_type=MESH)

    moves = (
        (item_factor_hbm, slabs.at[0]),
        (item_dual_hbm, slabs.at[1]),
        (user_factor_hbm, slabs.at[2]),
        (user_dual_hbm, slabs.at[3]),
        (time_factor_hbm, time_factor),
        (coords_hbm, coords),
        (user_owner_hbm, user_owner),
        (item_owner_hbm, item_owner),
        (act_hbm.at[0], act),
    )
    loads = [
        pltpu.make_async_copy(src, dst, load_sems.at[i]) for i, (src, dst) in enumerate(moves)
    ]
    for load in loads:
        load.start()

    groups = []

    class Group:
        def __init__(self, ref):
            k = 2 * len(groups)
            assert k + 1 < SEMS
            groups.append(self)
            self.whole = pltpu.make_async_remote_copy(
                src_ref=ref,
                dst_ref=ref,
                send_sem=sems.at[k],
                recv_sem=sems.at[k + 1],
                device_id=twin_dev,
                device_id_type=MESH,
            )
            self.pair = dict(send_sem=sems.at[k], recv_sem=sems.at[k + 1], device_id_type=MESH)

        def send(self, src, dst, device):
            pltpu.make_async_remote_copy(
                src_ref=src, dst_ref=dst, device_id=device, **self.pair
            ).start()

        def take(self):
            self.whole.wait_recv()

    def pack(which):
        stacked = jnp.concatenate(
            [slabs[which, :, t * 128 : (t + 1) * 128] for t in range(4)], axis=0
        )
        packed[which] = stacked.T

    def lines(place, size):
        return pl.ds(pl.multiple_of(place * size, size), size)

    def unpack(which):
        for t in range(4):
            held[which, t * 16 : (t + 1) * 16] = jnp.concatenate(
                [landed[which, n, :, t * 32 : (t + 1) * 32] for n in range(DEPTH)], axis=1
            )

    loads[0].wait()
    pack(0)
    pl.semaphore_wait(barrier, len(peers))
    lead = Group(landed.at[0, 0:7])
    for d in around:
        lead.send(packed.at[0, lines(z_at(d), 16)], landed.at[0, z], z_dev(d))
    landed[0, z] = packed[0, lines(z, 16)]
    for load in loads[1:8]:
        load.wait()
    for a in (1, 2, 3):
        pack(a)
        landed[a, z] = packed[a, lines(z, 16)]
    times = time_factor[...]
    time_gram = exact_dot(times.T, times)
    eye = (
        lax.broadcasted_iota(jnp.int32, (RANK, RANK), 0)
        == lax.broadcasted_iota(jnp.int32, (RANK, RANK), 1)
    ).astype(F32)
    lead.take()
    unpack(0)

    rest = Group(landed.at[1:4, 0:7])

    def send_rest():
        for d in around:
            rest.send(
                packed.at[1:4, lines(z_at(d), 16)], landed.at[1:4, z], z_dev(d)
            )

    def unpack_rest():
        rest.take()
        for a in (1, 2, 3):
            unpack(a)

    def gather(p, rows, after_start, after_middle):
        buf = gath.at[p]
        for h in range(2):
            buf[h, x, y, c] = rows[h * 32 : (h + 1) * 32].astype(BF16)
        starts = Group(buf.at[0, 0, 0:3])
        for d in (2, 1, 3):
            for h in range(2):
                starts.send(buf.at[h, x, y, c], buf.at[h, x, y, c], (x_dev, y_dev)[h](d))
        high = rows.astype(BF16)
        low = rows - high.astype(F32)
        missed = lax.dot_general(
            (high.astype(F32) + 0.5 * low).astype(BF16),
            low.astype(BF16),
            (((0,), (0,)), ((), ())),
            preferred_element_type=F32,
        )
        fix[p, 0:RANK] = (missed + missed.T).astype(BF16)
        fixes = Group(fix_land.at[p, :, 0:64])
        for d in (2, 1, 3):
            fixes.send(
                fix.at[p, lines(lax.rem(x + d, SIDE), 64)], fix_land.at[p, d - 1, 0:64], x_dev(d)
            )
        after_start()
        starts.take()
        middles = Group(buf.at[0, 0:3])
        mine = (buf.at[0, :, y, c], buf.at[1, x, :, c])
        for d in (2, 1, 3):
            for h in range(2):
                middles.send(mine[h], mine[h], (y_dev, x_dev)[h](d))
        fixes.take()
        total = fix[p, lines(x, 64)].astype(F32)
        for d in (1, 2, 3):
            total += fix_land[p, d - 1, 0:64].astype(F32)
        fix[p, RANK : RANK + 64] = total.astype(BF16)
        fixes = Group(fix_land.at[p, :, 64:80])
        for d in (2, 1, 3):
            fixes.send(
                fix.at[p, lines(lax.rem(y + d, SIDE) + 16, 16)],
                fix_land.at[p, d - 1, 64:80],
                y_dev(d),
            )
        after_middle()
        middles.take()
        twins = Group(buf.at[:, :, :, 0])
        for h in range(2):
            twins.send(buf.at[h, :, :, c], buf.at[h, :, :, c], twin_dev)
        fixes.take()
        total = fix[p, lines(y + 16, 16)].astype(F32)
        for d in (1, 2, 3):
            total += fix_land[p, d - 1, 64:80].astype(F32)
        fix[p, RANK + 64 : RANK + 80] = total.astype(BF16)
        fixes = Group(fix_land.at[p, 0, 80:96])
        fixes.send(fix.at[p, RANK + 64 : RANK + 80], fix_land.at[p, 0, 80:96], twin_dev)
        twins.take()
        fixes.take()

    def fetch(p, coord, owner):
        def choose(j):
            place = owner[coords[coord, wide * DEPTH + j]]
            spot = (place // 8, (place // 2) % SIDE, place % CORES)
            for h in range(2):
                zsend[p, j, 2 * h : 2 * h + 2] = gath[p, h, spot[0], spot[1], spot[2]].reshape(
                    2, 16, RANK
                )

        fetched = Group(kbuf.at[p, :, 0:7])
        for d in around:
            choose(z_at(d))
            fetched.send(zsend.at[p, z_at(d)], kbuf.at[p, :, z], z_dev(d))
        choose(z)
        kbuf[p, :, z] = zsend[p, z]
        return fetched

    def gram_start(p):
        total = jnp.zeros((RANK, RANK), F32)
        for h in range(2):
            for a in range(SIDE):
                some = gath[p, h, a].reshape(SIDE * CORES * 32, RANK)
                total += lax.dot_general(
                    some, some, (((0,), (0,)), ((), ())), preferred_element_type=F32
                )
        gpart[p] = total
        own = lines(wide, 8)
        both = fix[p, RANK + 64 : RANK + 80].astype(F32) + fix_land[p, 0, 80:96].astype(F32)
        gpart[p, own] += jnp.where(c == 0, both[0:8], both[8:16])
        group = Group(gland.at[p, 0:7])
        for d in around:
            group.send(gpart.at[p, own], gland.at[p, z], z_dev(d))
        gland[p, z] = gpart[p, own]
        return group

    def gram_sum(p, group):
        group.take()
        gfull[p, x, y, c] = jnp.sum(gland[p], axis=0)
        spot = gfull.at[p, x, y, c]
        group = Group(gfull.at[p, 0, 0:3, 0])
        for d in (2, 1, 3):
            group.send(spot, spot, x_dev(d))
        return group

    def gram_line(p, group):
        group.take()
        line = gfull.at[p, :, y, c]
        group = Group(gfull.at[p, 0:3, :, 0])
        for d in (2, 1, 3):
            group.send(line, line, y_dev(d))
        return group

    def gram_plane(p, group):
        group.take()
        plane = gfull.at[p, :, :, c]
        group = Group(gfull.at[p, :, :, 0])
        group.send(plane, plane, twin_dev)
        return group

    def inverse_start(p, group):
        group.take()
        gram = gfull[p].reshape(RANK, RANK) * time_gram
        penalty = jnp.sum(gram * eye) / RANK
        base[...] = gram / penalty + eye
        t = SCALES[0]
        gain = 2.0 * t * t / (2.0 * t * t - 1.0)
        approx[...] = (eye * 2.0 - base[...] * (1.0 / 129.0)) * (gain / 129.0)
        return penalty

    def inverse_steps(first, last):
        def step(_, t):
            t2 = 2.0 * t * t - 1.0
            now = approx[...]
            error = eye - exact_dot(base[...], now)
            approx[...] = (now + exact_dot(now, error)) * ((t2 + 1.0) / t2)
            return t2

        lax.fori_loop(first, last, step, F32(SCALES[first + 1]))

    def tile_half(p, h, forward, khatri_t):
        total = jnp.zeros((BLOCK // 2, RANK), F32)
        cut = slice(h * 256, (h + 1) * 256)
        for k in range(TIMES):
            if forward:
                total += jnp.dot(act[k, cut, :], khatri[k], preferred_element_type=F32)
            else:
                total += jnp.dot(khatri_t[k], act[k, :, cut], preferred_element_type=F32)
        if not forward:
            total = total.T
        partial[p, 2 * h : 2 * h + 2] = total.reshape(2, DEPTH, 16, RANK)
        pair = pl.ds(2 * h, 2)
        group = Group(tland.at[p, h, 0:7])
        for d in around:
            group.send(partial.at[p, pair, z_at(d)], tland.at[p, h, z], z_dev(d))
        tland[p, h, z] = partial[p, 2 * h : 2 * h + 2, z]
        return group

    def reduced(p, coord, owner, arrived, gram):
        targets = [owner[coords[coord, wide * DEPTH + j]] for j in range(DEPTH)]
        twin_targets = [owner[coords[coord, twin * DEPTH + j]] for j in range(DEPTH)]

        def pass_on(h):
            arrived[h].take()
            twins = Group(cland.at[p, h])
            twins.send(tland.at[p, h], cland.at[p, h], twin_dev)
            return twins

        def spread(h, twins):
            twins.take()
            firsts = [Group(first_land.at[p, h, v]) for v in range(2)]
            for d in (2, 1, 3, 0):
                for v in range(2):
                    a = lax.rem((x, y)[v] + d, SIDE)
                    cut = slice(v * 128, (v + 1) * 128)

                    def place(b, carry):
                        block = ((a * SIDE + b) if v == 0 else (b * SIDE + a)) * CORES + c
                        total = jnp.zeros((2, 16, 128), F32)
                        for j in range(DEPTH):
                            total += tland[p, h, j, :, :, cut] * (targets[j] == block).astype(F32)
                            total += cland[p, h, j, :, :, cut] * (
                                twin_targets[j] == block
                            ).astype(F32)
                        dense[p, h, v, a, b] = total
                        return carry

                    lax.fori_loop(0, SIDE, place, 0)
                    if d:
                        firsts[v].send(
                            dense.at[p, h, v, a],
                            first_land.at[p, h, v, d - 1],
                            (x_dev, y_dev)[v](d),
                        )
            return firsts

        def spread_on(h, firsts):
            seconds = [Group(last_land.at[p, h, v]) for v in range(2)]
            for v in range(2):
                firsts[v].take()
                middle[p, h, v] = (dense[p, h, v, (x, y)[v]] + first_land[p, h, v, 0]) + (
                    first_land[p, h, v, 1] + first_land[p, h, v, 2]
                )
                for d in (2, 1, 3):
                    seconds[v].send(
                        middle.at[p, h, v, lax.rem((y, x)[v] + d, SIDE)],
                        last_land.at[p, h, v, d - 1],
                        (y_dev, x_dev)[v](d),
                    )
            return seconds

        def finish(h, seconds):
            parts = []
            for v in range(2):
                seconds[v].take()
                total = (middle[p, h, v, (y, x)[v]] + last_land[p, h, v, 0]) + (
                    last_land[p, h, v, 1] + last_land[p, h, v, 2]
                )
                parts.append(total.reshape(32, 128))
            return jnp.concatenate(parts, axis=1)

        gram = gram_sum(p, gram)
        twins = [pass_on(0)]
        gram = gram_line(p, gram)
        firsts = [spread(0, twins[0])]
        gram = gram_plane(p, gram)
        penalty = inverse_start(p, gram)
        inverse_steps(0, 2)
        twins.append(pass_on(1))
        seconds = [spread_on(0, firsts[0])]
        firsts.append(spread(1, twins[1]))
        inverse_steps(2, 5)
        seconds.append(spread_on(1, firsts[1]))
        inverse_steps(5, STEPS)
        return jnp.concatenate([finish(h, seconds[h]) for h in range(2)], axis=0), penalty

    def admm(sums, factor, dual, penalty):
        inverse = approx[...]
        for _ in range(PASSES):
            target = exact_dot(sums + penalty * (factor + dual), inverse) / penalty
            factor = jnp.maximum(target - dual, 0.0)
            dual = dual + factor - target
        return factor, dual

    def give_back(p, factor, dual):
        for a, rows in ((0, factor), (1, dual)):
            for n in range(DEPTH):
                opack[p, n, a] = jnp.concatenate(
                    [
                        rows[t * 16 : (t + 1) * 16, n * 32 : (n + 1) * 32]
                        for t in range(4)
                    ],
                    axis=1,
                )
        group = Group(oland.at[p, :, 0:7])
        for d in around:
            group.send(opack.at[p, z_at(d)], oland.at[p, :, z], z_dev(d))
        oland[p, :, z] = opack[p, z]
        return group

    def take_back(p, group, outs):
        group.take()
        for a in range(2):
            turned = oland[p, a].reshape(128, 128).T
            for t in range(4):
                outs[a][:, t * 128 : (t + 1) * 128] = turned[t * 32 : (t + 1) * 32, :]

    def update(p, rows, factor_at, dual_at, own_coord, own, other, after_start, after_middle, after_gram):
        forward = p == 0
        gather(p, rows, after_start, after_middle)
        fetched = fetch(p, 1 - own_coord, other)
        gram = gram_start(p)
        after_gram()
        fetched.take()
        if forward:
            loads[8].wait()
        low = kbuf[p].reshape(BLOCK, RANK).astype(F32)
        khatri_t = None
        if forward:
            for k in range(TIMES):
                khatri[k] = (low * times[k : k + 1, :]).astype(BF16)
        else:
            turned = low.T
            columns = times.T
            khatri_t = [(turned * columns[:, k : k + 1]).astype(BF16) for k in range(TIMES)]
        arrived = [tile_half(p, h, forward, khatri_t) for h in range(2)]
        sums, penalty = reduced(p, own_coord, own, arrived, gram)
        return admm(sums, held[factor_at], held[dual_at], penalty)

    nothing = lambda: None
    users, user_duals = update(
        0, held[0], 2, 3, 0, user_owner, item_owner, send_rest, unpack_rest, nothing
    )
    returned = []
    items, item_duals = update(
        1,
        users,
        0,
        1,
        1,
        item_owner,
        user_owner,
        nothing,
        lambda: returned.append(give_back(0, users, user_duals)),
        lambda: take_back(0, returned[0], (out_users, out_user_duals)),
    )
    take_back(1, give_back(1, items, item_duals), (out_items, out_item_duals))
    for group in groups:
        group.whole.wait_send()


def settle_kernel(*refs):
    for a in range(4):
        refs[4 + a][...] = refs[a][...]


def local(
    activity,
    tile_coords,
    user_owner,
    item_owner,
    user_factor,
    item_factor,
    time_factor,
    user_dual,
    item_dual,
):
    hbm = pl.BlockSpec(memory_space=pltpu.HBM)
    vmem = pl.BlockSpec(memory_space=pltpu.VMEM)
    slab = jax.ShapeDtypeStruct((RANK // DEPTH, BLOCK), F32)
    outs = pl.pallas_call(
        sweep_kernel,
        out_shape=(slab,) * 4,
        in_specs=[hbm] * 9,
        out_specs=(vmem,) * 4,
        scratch_shapes=[
            pltpu.VMEM((TIMES, BLOCK, BLOCK), BF16),
            pltpu.SMEM((2, RANK), jnp.int32),
            pltpu.SMEM((32,), jnp.int32),
            pltpu.SMEM((32,), jnp.int32),
            pltpu.VMEM((4, RANK // DEPTH, BLOCK), F32),
            pltpu.VMEM((TIMES, RANK), F32),
            pltpu.VMEM((4, 128, 128), F32),
            pltpu.VMEM((4, DEPTH, 16, 128), F32),
            pltpu.VMEM((4, 64, RANK), F32),
            pltpu.VMEM((TIMES, BLOCK, RANK), BF16),
            pltpu.VMEM((2, 2, SIDE, SIDE, CORES, 32, RANK), BF16),
            pltpu.VMEM((2, DEPTH, 4, 16, RANK), BF16),
            pltpu.VMEM((2, 4, DEPTH, 16, RANK), BF16),
            pltpu.VMEM((2, RANK, RANK), F32),
            pltpu.VMEM((2, RANK + 80, RANK), BF16),
            pltpu.VMEM((2, SIDE - 1, 96, RANK), BF16),
            pltpu.VMEM((2, DEPTH, 8, RANK), F32),
            pltpu.VMEM((2, SIDE, SIDE, CORES, 8, RANK), F32),
            pltpu.VMEM((RANK, RANK), F32),
            pltpu.VMEM((RANK, RANK), F32),
            pltpu.VMEM((2, 4, DEPTH, 16, RANK), F32),
            pltpu.VMEM((2, 2, DEPTH, 2, 16, RANK), F32),
            pltpu.VMEM((2, 2, DEPTH, 2, 16, RANK), F32),
            pltpu.VMEM((2, 2, 2, SIDE, SIDE, 2, 16, 128), F32),
            pltpu.VMEM((2, 2, 2, SIDE - 1, SIDE, 2, 16, 128), F32),
            pltpu.VMEM((2, 2, 2, SIDE, 2, 16, 128), F32),
            pltpu.VMEM((2, 2, 2, SIDE - 1, 2, 16, 128), F32),
            pltpu.VMEM((2, DEPTH, 2, 16, 128), F32),
            pltpu.VMEM((2, 2, DEPTH, 16, 128), F32),
            pltpu.SemaphoreType.DMA((SEMS,)),
            pltpu.SemaphoreType.DMA((9,)),
        ],
        compiler_params=pltpu.CompilerParams(
            collective_id=0, has_side_effects=True, vmem_limit_bytes=56 * 2**20
        ),
        name="sweep",
    )(
        activity,
        tile_coords.T,
        user_owner,
        item_owner,
        user_factor.T,
        item_factor.T,
        time_factor,
        user_dual.T,
        item_dual.T,
    )
    outs = pl.pallas_call(settle_kernel, out_shape=(slab,) * 4, name="settle")(*outs)
    users, items, user_duals, item_duals = (out.T for out in outs)
    return (users, items, user_duals, item_duals)


def solution(mesh):
    split = Mesh(
        mesh.devices.reshape(SIDE, SIDE, CORES, mesh.shape["narrow"]),
        WIDE_NARROW,
    )
    in_specs = (
        P(WIDE_NARROW, None, None, None),
        P(),
        P(),
        P(),
        P(WIDE, "narrow"),
        P(WIDE, "narrow"),
        P(),
        P(WIDE, "narrow"),
        P(WIDE, "narrow"),
    )
    out_specs = (P(WIDE, "narrow"), P(WIDE, "narrow"), P(WIDE, "narrow"), P(WIDE, "narrow"))
    return jax.shard_map(local, mesh=split, in_specs=in_specs, out_specs=out_specs, check_vma=False)
```

```python
import jax
import jax.numpy as jnp
from jax import lax
from jax.experimental import pallas as pl
from jax.experimental.pallas import tpu as pltpu
from jax.sharding import Mesh
from jax.sharding import PartitionSpec as P

RANK = 256
BLOCK = 512
TIMES = 8
PASSES = 2
SIDE = 4
CORES = 2
DEPTH = 8
STEPS = 6
SCALES = [129.0 / 128.0]
for _ in range(STEPS):
    SCALES.append(2.0 * SCALES[-1] ** 2 - 1.0)
MESH = pl.DeviceIdType.MESH
WIDE = ("wide_0", "wide_1", "wide_2")
WIDE_NARROW = ("wide_0", "wide_1", "wide_2", "narrow")
SEMS = 104
F32 = jnp.float32
BF16 = jnp.bfloat16


def exact_dot(a, b):
    return jnp.dot(a, b, precision=lax.Precision.HIGHEST, preferred_element_type=F32)


def sweep_kernel(
    act_hbm,
    coords_hbm,
    user_owner_hbm,
    item_owner_hbm,
    user_factor_hbm,
    item_factor_hbm,
    time_factor_hbm,
    user_dual_hbm,
    item_dual_hbm,
    out_users,
    out_items,
    out_user_duals,
    out_item_duals,
    act,
    coords,
    user_owner,
    item_owner,
    slabs,
    time_factor,
    packed,
    landed,
    held,
    khatri,
    gath,
    zsend,
    kbuf,
    gpart,
    xland,
    yland,
    high_part,
    fix,
    fix_land,
    gland,
    gfull,
    base,
    approx,
    partial,
    tland,
    cland,
    dense,
    first_land,
    middle,
    last_land,
    opack,
    oland,
    sems,
    load_sems,
):
    x, y, c, z = (lax.axis_index(name) for name in WIDE_NARROW)
    wide = (x * SIDE + y) * CORES + c
    twin = (x * SIDE + y) * CORES + (1 - c)
    twin_dev = (x, y, 1 - c, z)

    def x_dev(d):
        return (lax.rem(x + d, SIDE), y, c, z)

    def y_dev(d):
        return (x, lax.rem(y + d, SIDE), c, z)

    def z_at(d):
        return lax.rem(z + d, DEPTH)

    def z_dev(d):
        return (x, y, c, z_at(d))

    around = (4, 3, 5, 2, 6, 1, 7)

    barrier = pltpu.get_barrier_semaphore()
    peers = [x_dev(d) for d in (1, 2, 3)] + [y_dev(d) for d in (1, 2, 3)]
    peers += [z_dev(d) for d in range(1, DEPTH)] + [twin_dev]
    for peer in peers:
        pl.semaphore_signal(barrier, inc=1, device_id=peer, device_id_type=MESH)

    moves = (
        (item_factor_hbm, slabs.at[0]),
        (item_dual_hbm, slabs.at[1]),
        (user_factor_hbm, slabs.at[2]),
        (user_dual_hbm, slabs.at[3]),
        (time_factor_hbm, time_factor),
        (coords_hbm, coords),
        (user_owner_hbm, user_owner),
        (item_owner_hbm, item_owner),
        (act_hbm.at[0], act),
    )
    loads = [
        pltpu.make_async_copy(src, dst, load_sems.at[i]) for i, (src, dst) in enumerate(moves)
    ]
    for load in loads:
        load.start()

    groups = []

    class Group:
        def __init__(self, ref):
            k = 2 * len(groups)
            assert k + 1 < SEMS
            groups.append(self)
            self.whole = pltpu.make_async_remote_copy(
                src_ref=ref,
                dst_ref=ref,
                send_sem=sems.at[k],
                recv_sem=sems.at[k + 1],
                device_id=twin_dev,
                device_id_type=MESH,
            )
            self.pair = dict(send_sem=sems.at[k], recv_sem=sems.at[k + 1], device_id_type=MESH)

        def send(self, src, dst, device):
            pltpu.make_async_remote_copy(
                src_ref=src, dst_ref=dst, device_id=device, **self.pair
            ).start()

        def take(self):
            self.whole.wait_recv()

    def pack(which):
        stacked = jnp.concatenate(
            [slabs[which, :, t * 128 : (t + 1) * 128] for t in range(4)], axis=0
        )
        packed[which] = stacked.T

    def lines(place, size):
        return pl.ds(pl.multiple_of(place * size, size), size)

    def unpack(which):
        for t in range(4):
            held[which, t * 16 : (t + 1) * 16] = jnp.concatenate(
                [landed[which, n, :, t * 32 : (t + 1) * 32] for n in range(DEPTH)], axis=1
            )

    loads[0].wait()
    pl.semaphore_wait(barrier, len(peers))

    rows_group = Group(landed.at[:, 0:7])

    def send_rows():
        for load in loads[1:8]:
            load.wait()
        for a in range(4):
            pack(a)
            landed[a, z] = packed[a, lines(z, 16)]
        for d in around:
            rows_group.send(packed.at[:, lines(z_at(d), 16)], landed.at[:, z], z_dev(d))

    def take_rows():
        rows_group.take()
        for a in range(4):
            unpack(a)

    def gather(p, halves, after_start, after_middle, after_plane):
        buf = gath.at[p]
        own = (buf.at[0, c, y, x], buf.at[1, c, x, y])
        for h in range(2):
            own[h][...] = halves[h].astype(BF16)
        starts = Group(buf.at[0, 0, 0:2, 0:3])
        for d in (2, 1, 3):
            for h in range(2):
                starts.send(own[h], own[h], (x_dev, y_dev)[h](d))
        after_start()
        starts.take()
        middles = Group(buf.at[:, 0, 0:3])
        mine = (buf.at[0, c, y], buf.at[1, c, x])
        for d in (2, 1, 3):
            for h in range(2):
                middles.send(mine[h], mine[h], (y_dev, x_dev)[h](d))
        after_middle()
        middles.take()
        twins = Group(buf.at[:, 0])
        for h in range(2):
            twins.send(buf.at[h, c], buf.at[h, c], twin_dev)
        after_plane()
        twins.take()

    def fetch(p, coord, owner):
        def choose(j):
            place = owner[coords[coord, wide * DEPTH + j]]
            a, b, core = place // 8, (place // 2) % SIDE, place % CORES
            zsend[p, j, 0:2] = gath[p, 0, core, b, a].reshape(2, 16, RANK)
            zsend[p, j, 2:4] = gath[p, 1, core, a, b].reshape(2, 16, RANK)

        fetched = Group(kbuf.at[p, 0:7])
        for d in around:
            choose(z_at(d))
            fetched.send(zsend.at[p, z_at(d)], kbuf.at[p, z], z_dev(d))
        choose(z)
        kbuf[p, z] = zsend[p, z]
        return fetched

    def gram_local(p, rows):
        gpart[p, 0:RANK] = exact_dot(rows.T, rows)

    def gram_x(p):
        group = Group(xland.at[p])
        for d in (2, 1, 3):
            group.send(
                gpart.at[p, lines(lax.rem(x + d, SIDE), 64)], xland.at[p, d - 1], x_dev(d)
            )
        return group

    def gram_y(p, group):
        group.take()
        gpart[p, RANK : RANK + 64] = (gpart[p, lines(x, 64)] + xland[p, 0]) + (
            xland[p, 1] + xland[p, 2]
        )
        group = Group(yland.at[p, 0:3])
        for d in (2, 1, 3):
            group.send(
                gpart.at[p, lines(lax.rem(y + d, SIDE) + 16, 16)], yland.at[p, d - 1], y_dev(d)
            )
        return group

    def gram_twin(p, group):
        group.take()
        gpart[p, RANK + 64 : RANK + 80] = (gpart[p, lines(y + 16, 16)] + yland[p, 0]) + (
            yland[p, 1] + yland[p, 2]
        )
        group = Group(yland.at[p, 3])
        group.send(gpart.at[p, RANK + 64 : RANK + 80], yland.at[p, 3], twin_dev)
        return group

    def gram_z(p, group):
        group.take()
        both = gpart[p, RANK + 64 : RANK + 80] + yland[p, 3]
        gpart[p, RANK + 80 : RANK + 88] = jnp.where(c == 0, both[0:8], both[8:16])
        group = Group(gland.at[p, 0:7])
        for d in around:
            group.send(gpart.at[p, RANK + 80 : RANK + 88], gland.at[p, z], z_dev(d))
        gland[p, z] = gpart[p, RANK + 80 : RANK + 88]
        return group

    def fix_local(rows):
        high = rows.astype(BF16)
        low = rows - high.astype(F32)
        missed = lax.dot_general(
            (high.astype(F32) + 0.5 * low).astype(BF16),
            low.astype(BF16),
            (((0,), (0,)), ((), ())),
            preferred_element_type=F32,
        )
        fix[0:RANK] = (missed + missed.T).astype(BF16)

    def fix_x():
        group = Group(fix_land.at[:, 0:64])
        for d in (2, 1, 3):
            group.send(
                fix.at[lines(lax.rem(x + d, SIDE), 64)], fix_land.at[d - 1, 0:64], x_dev(d)
            )
        return group

    def fix_y(group):
        group.take()
        total = fix[lines(x, 64)].astype(F32)
        for d in (1, 2, 3):
            total += fix_land[d - 1, 0:64].astype(F32)
        fix[RANK : RANK + 64] = total.astype(BF16)
        group = Group(fix_land.at[:, 64:80])
        for d in (2, 1, 3):
            group.send(
                fix.at[lines(lax.rem(y + d, SIDE) + 16, 16)], fix_land.at[d - 1, 64:80], y_dev(d)
            )
        return group

    def fix_twin(group):
        group.take()
        total = fix[lines(y + 16, 16)].astype(F32)
        for d in (1, 2, 3):
            total += fix_land[d - 1, 64:80].astype(F32)
        fix[RANK + 64 : RANK + 80] = total.astype(BF16)
        group = Group(fix_land.at[0, 80:96])
        group.send(fix.at[RANK + 64 : RANK + 80], fix_land.at[0, 80:96], twin_dev)
        return group

    def gram_high(p, group):
        total = jnp.zeros((RANK, RANK), F32)
        for h in range(2):
            for a in range(SIDE):
                some = gath[p, h, a // 2, (a % 2) * 2 : (a % 2) * 2 + 2].reshape(256, RANK)
                total += lax.dot_general(
                    some, some, (((0,), (0,)), ((), ())), preferred_element_type=F32
                )
        high_part[...] = total
        group.take()
        own = lines(wide, 8)
        both = fix[RANK + 64 : RANK + 80].astype(F32) + fix_land[0, 80:96].astype(F32)
        high_part[own] += jnp.where(c == 0, both[0:8], both[8:16])
        group = Group(gland.at[p, 0:7])
        for d in around:
            group.send(high_part.at[own], gland.at[p, z], z_dev(d))
        gland[p, z] = high_part[own]
        return group

    def gram_sum(p, group):
        group.take()
        spot = gfull.at[p, c, y, x]
        spot[...] = jnp.sum(gland[p], axis=0)
        group = Group(gfull.at[p, 0, 0, 0:3])
        for d in (2, 1, 3):
            group.send(spot, spot, x_dev(d))
        return group

    def gram_line(p, group):
        group.take()
        line = gfull.at[p, c, y]
        group = Group(gfull.at[p, 0, 0:3])
        for d in (2, 1, 3):
            group.send(line, line, y_dev(d))
        return group

    def gram_plane(p, group):
        group.take()
        plane = gfull.at[p, c]
        group = Group(gfull.at[p, 0])
        group.send(plane, plane, twin_dev)
        return group

    def inverse_start(p, group):
        group.take()
        gram = gfull[p].transpose(2, 1, 0, 3, 4).reshape(RANK, RANK) * time_gram
        penalty = jnp.sum(gram * eye) / RANK
        base[...] = gram / penalty + eye
        t = SCALES[0]
        gain = 2.0 * t * t / (2.0 * t * t - 1.0)
        approx[...] = (eye * 2.0 - base[...] * (1.0 / 129.0)) * (gain / 129.0)
        return penalty

    def split(a):
        high = a.astype(BF16)
        return high, (a - high.astype(F32)).astype(BF16)

    def near_dot(a, b):
        (ah, al), (bh, bl) = split(a), split(b)
        return (
            jnp.dot(ah, bl, preferred_element_type=F32)
            + jnp.dot(al, bh, preferred_element_type=F32)
        ) + jnp.dot(ah, bh, preferred_element_type=F32)

    def inverse_steps(first, last):
        dot = near_dot if last < STEPS else exact_dot

        def step(_, t):
            t2 = 2.0 * t * t - 1.0
            now = approx[...]
            error = eye - dot(base[...], now)
            approx[...] = (now + dot(now, error)) * ((t2 + 1.0) / t2)
            return t2

        lax.fori_loop(first, last, step, F32(SCALES[first + 1]))

    def tile_half(p, h, forward, khatri_t):
        total = jnp.zeros((BLOCK // 2, RANK), F32)
        cut = slice(h * 256, (h + 1) * 256)
        for k in range(TIMES):
            if forward:
                total += jnp.dot(act[k, cut, :], khatri[k], preferred_element_type=F32)
            else:
                total += jnp.dot(khatri_t[k], act[k, :, cut], preferred_element_type=F32)
        if not forward:
            total = total.T
        partial[p, h] = total.reshape(2, DEPTH, 16, RANK).swapaxes(0, 1)
        group = Group(tland.at[p, h, 0:7])
        for d in around:
            group.send(partial.at[p, h, z_at(d)], tland.at[p, h, z], z_dev(d))
        tland[p, h, z] = partial[p, h, z]
        return group

    def reduced(p, coord, owner, arrived, gram):
        targets = [owner[coords[coord, wide * DEPTH + j]] for j in range(DEPTH)]
        twin_targets = [owner[coords[coord, twin * DEPTH + j]] for j in range(DEPTH)]

        def pass_on(h):
            arrived[h].take()
            twins = Group(cland.at[p, h])
            twins.send(tland.at[p, h], cland.at[p, h], twin_dev)
            return twins

        def spread(h, twins):
            twins.take()
            firsts = [Group(first_land.at[p, h, v]) for v in range(2)]
            for d in (2, 1, 3, 0):
                for v in range(2):
                    a = lax.rem((x, y)[v] + d, SIDE)
                    cut = slice(v * 128, (v + 1) * 128)

                    def place(b, carry):
                        block = ((a * SIDE + b) if v == 0 else (b * SIDE + a)) * CORES + c
                        total = jnp.zeros((2, 16, 128), F32)
                        for j in range(DEPTH):
                            total += tland[p, h, j, :, :, cut] * (targets[j] == block).astype(F32)
                            total += cland[p, h, j, :, :, cut] * (
                                twin_targets[j] == block
                            ).astype(F32)
                        dense[p, h, v, a, b] = total
                        return carry

                    lax.fori_loop(0, SIDE, place, 0)
                    if d:
                        firsts[v].send(
                            dense.at[p, h, v, a],
                            first_land.at[p, h, v, d - 1],
                            (x_dev, y_dev)[v](d),
                        )
            return firsts

        def spread_on(h, firsts):
            seconds = [Group(last_land.at[p, h, v]) for v in range(2)]
            for v in range(2):
                firsts[v].take()
                middle[p, h, v] = (dense[p, h, v, (x, y)[v]] + first_land[p, h, v, 0]) + (
                    first_land[p, h, v, 1] + first_land[p, h, v, 2]
                )
                for d in (2, 1, 3):
                    seconds[v].send(
                        middle.at[p, h, v, lax.rem((y, x)[v] + d, SIDE)],
                        last_land.at[p, h, v, d - 1],
                        (y_dev, x_dev)[v](d),
                    )
            return seconds

        def finish(h, seconds):
            parts = []
            for v in range(2):
                seconds[v].take()
                total = (middle[p, h, v, (y, x)[v]] + last_land[p, h, v, 0]) + (
                    last_land[p, h, v, 1] + last_land[p, h, v, 2]
                )
                parts.append(total.reshape(32, 128))
            return jnp.concatenate(parts, axis=1)

        gram = gram_sum(p, gram)
        twins = [pass_on(0)]
        gram = gram_line(p, gram)
        firsts = [spread(0, twins[0])]
        gram = gram_plane(p, gram)
        penalty = inverse_start(p, gram)
        inverse_steps(0, 2)
        twins.append(pass_on(1))
        seconds = [spread_on(0, firsts[0])]
        inverse_steps(2, 3)
        firsts.append(spread(1, twins[1]))
        inverse_steps(3, 4)
        seconds.append(spread_on(1, firsts[1]))
        inverse_steps(4, STEPS)
        return jnp.concatenate([finish(h, seconds[h]) for h in range(2)], axis=0), penalty

    def admm(sums, factor, dual, penalty):
        inverse = approx[...]
        for _ in range(PASSES):
            target = exact_dot(sums + penalty * (factor + dual), inverse) / penalty
            factor = jnp.maximum(target - dual, 0.0)
            dual = dual + factor - target
        return factor, dual

    def give_back(p, factor, dual):
        for a, rows in ((0, factor), (1, dual)):
            for n in range(DEPTH):
                opack[p, n, a] = jnp.concatenate(
                    [
                        rows[t * 16 : (t + 1) * 16, n * 32 : (n + 1) * 32]
                        for t in range(4)
                    ],
                    axis=1,
                )
        group = Group(oland.at[p, :, 0:7])
        for d in around:
            group.send(opack.at[p, z_at(d)], oland.at[p, :, z], z_dev(d))
        oland[p, :, z] = opack[p, z]
        return group

    def take_back(p, group, outs):
        group.take()
        for a in range(2):
            turned = oland[p, a].reshape(128, 128).T
            for t in range(4):
                outs[a][:, t * 128 : (t + 1) * 128] = turned[t * 32 : (t + 1) * 32, :]

    nothing = lambda: None

    def table(p, low):
        if p == 0:
            for k in range(TIMES):
                khatri[k] = (low * times[k : k + 1, :]).astype(BF16)
            return None
        turned = low.T
        columns = times.T
        return [(turned * columns[:, k : k + 1]).astype(BF16) for k in range(TIMES)]

    gather(
        0,
        [slabs[0, :, 0:256], slabs[0, :, 256:512]],
        nothing,
        send_rows,
        nothing,
    )
    fetched = fetch(0, 1, item_owner)
    times = time_factor[...]
    time_gram = exact_dot(times.T, times)
    eye = (
        lax.broadcasted_iota(jnp.int32, (RANK, RANK), 0)
        == lax.broadcasted_iota(jnp.int32, (RANK, RANK), 1)
    ).astype(F32)
    take_rows()
    gram_local(0, held[0])
    gram = gram_twin(0, gram_y(0, gram_x(0)))
    fetched.take()
    loads[8].wait()
    turned = jnp.concatenate(
        [kbuf[0, :, 2 * h : 2 * h + 2].reshape(RANK, 256) for h in range(2)], axis=1
    )
    table(0, turned.astype(F32).T)
    gram = gram_z(0, gram)
    arrived = [tile_half(0, h, True, None) for h in range(2)]
    sums, penalty = reduced(0, 0, user_owner, arrived, gram)
    users, user_duals = admm(sums, held[2], held[3], penalty)

    returned = []
    grams = []
    gather(
        1,
        [users[0:32], users[32:64]],
        lambda: (fix_local(users), grams.append(fix_x())),
        lambda: (
            grams.append(fix_y(grams[0])),
            returned.append(give_back(0, users, user_duals)),
        ),
        lambda: grams.append(fix_twin(grams[1])),
    )
    fetched = fetch(1, 0, user_owner)
    gram = gram_high(1, grams[2])
    take_back(0, returned[0], (out_users, out_user_duals))
    fetched.take()
    khatri_t = table(1, kbuf[1].swapaxes(0, 1).reshape(BLOCK, RANK).astype(F32))
    arrived = [tile_half(1, h, False, khatri_t) for h in range(2)]
    sums, penalty = reduced(1, 1, item_owner, arrived, gram)
    items, item_duals = admm(sums, held[0], held[1], penalty)
    take_back(1, give_back(1, items, item_duals), (out_items, out_item_duals))
    for group in groups:
        group.whole.wait_send()


def settle_kernel(*refs):
    for a in range(4):
        refs[4 + a][...] = refs[a][...]


def local(
    activity,
    tile_coords,
    user_owner,
    item_owner,
    user_factor,
    item_factor,
    time_factor,
    user_dual,
    item_dual,
):
    hbm = pl.BlockSpec(memory_space=pltpu.HBM)
    vmem = pl.BlockSpec(memory_space=pltpu.VMEM)
    slab = jax.ShapeDtypeStruct((RANK // DEPTH, BLOCK), F32)
    outs = pl.pallas_call(
        sweep_kernel,
        out_shape=(slab,) * 4,
        in_specs=[hbm] * 9,
        out_specs=(vmem,) * 4,
        scratch_shapes=[
            pltpu.VMEM((TIMES, BLOCK, BLOCK), BF16),
            pltpu.SMEM((2, RANK), jnp.int32),
            pltpu.SMEM((32,), jnp.int32),
            pltpu.SMEM((32,), jnp.int32),
            pltpu.VMEM((4, RANK // DEPTH, BLOCK), F32),
            pltpu.VMEM((TIMES, RANK), F32),
            pltpu.VMEM((4, 128, 128), F32),
            pltpu.VMEM((4, DEPTH, 16, 128), F32),
            pltpu.VMEM((4, 64, RANK), F32),
            pltpu.VMEM((TIMES, BLOCK, RANK), BF16),
            pltpu.VMEM((2, 2, CORES, SIDE, SIDE, 32, RANK), BF16),
            pltpu.VMEM((2, DEPTH, 4, 16, RANK), BF16),
            pltpu.VMEM((2, DEPTH, 4, 16, RANK), BF16),
            pltpu.VMEM((1, RANK + 88, RANK), F32),
            pltpu.VMEM((1, SIDE - 1, 64, RANK), F32),
            pltpu.VMEM((1, SIDE, 16, RANK), F32),
            pltpu.VMEM((RANK, RANK), F32),
            pltpu.VMEM((RANK + 80, RANK), BF16),
            pltpu.VMEM((SIDE - 1, 96, RANK), BF16),
            pltpu.VMEM((2, DEPTH, 8, RANK), F32),
            pltpu.VMEM((2, CORES, SIDE, SIDE, 8, RANK), F32),
            pltpu.VMEM((RANK, RANK), F32),
            pltpu.VMEM((RANK, RANK), F32),
            pltpu.VMEM((2, 2, DEPTH, 2, 16, RANK), F32),
            pltpu.VMEM((2, 2, DEPTH, 2, 16, RANK), F32),
            pltpu.VMEM((2, 2, DEPTH, 2, 16, RANK), F32),
            pltpu.VMEM((2, 2, 2, SIDE, SIDE, 2, 16, 128), F32),
            pltpu.VMEM((2, 2, 2, SIDE - 1, SIDE, 2, 16, 128), F32),
            pltpu.VMEM((2, 2, 2, SIDE, 2, 16, 128), F32),
            pltpu.VMEM((2, 2, 2, SIDE - 1, 2, 16, 128), F32),
            pltpu.VMEM((2, DEPTH, 2, 16, 128), F32),
            pltpu.VMEM((2, 2, DEPTH, 16, 128), F32),
            pltpu.SemaphoreType.DMA((SEMS,)),
            pltpu.SemaphoreType.DMA((9,)),
        ],
        compiler_params=pltpu.CompilerParams(
            collective_id=0, has_side_effects=True, vmem_limit_bytes=56 * 2**20
        ),
        name="sweep",
    )(
        activity,
        tile_coords.T,
        user_owner,
        item_owner,
        user_factor.T,
        item_factor.T,
        time_factor,
        user_dual.T,
        item_dual.T,
    )
    outs = pl.pallas_call(settle_kernel, out_shape=(slab,) * 4, name="settle")(*outs)
    users, items, user_duals, item_duals = (out.T for out in outs)
    return (users, items, user_duals, item_duals)


def solution(mesh):
    split = Mesh(
        mesh.devices.reshape(SIDE, SIDE, CORES, mesh.shape["narrow"]),
        WIDE_NARROW,
    )
    in_specs = (
        P(WIDE_NARROW, None, None, None),
        P(),
        P(),
        P(),
        P(WIDE, "narrow"),
        P(WIDE, "narrow"),
        P(),
        P(WIDE, "narrow"),
        P(WIDE, "narrow"),
    )
    out_specs = (P(WIDE, "narrow"), P(WIDE, "narrow"), P(WIDE, "narrow"), P(WIDE, "narrow"))
    return jax.shard_map(local, mesh=split, in_specs=in_specs, out_specs=out_specs, check_vma=False)
```

```python
import jax
import jax.numpy as jnp
from jax import lax
from jax.experimental import pallas as pl
from jax.experimental.pallas import tpu as pltpu
from jax.sharding import Mesh
from jax.sharding import PartitionSpec as P

RANK = 256
BLOCK = 512
TIMES = 8
PASSES = 2
SIDE = 4
CORES = 2
DEPTH = 8
STEPS = 6
SCALES = [129.0 / 128.0]
for _ in range(STEPS):
    SCALES.append(2.0 * SCALES[-1] ** 2 - 1.0)
MESH = pl.DeviceIdType.MESH
WIDE = ("wide_0", "wide_1", "wide_2")
WIDE_NARROW = ("wide_0", "wide_1", "wide_2", "narrow")
SEMS = 104
F32 = jnp.float32
BF16 = jnp.bfloat16


def exact_dot(a, b):
    return jnp.dot(a, b, precision=lax.Precision.HIGHEST, preferred_element_type=F32)


def sweep_kernel(
    act_hbm,
    coords_hbm,
    user_owner_hbm,
    item_owner_hbm,
    user_factor_hbm,
    item_factor_hbm,
    time_factor_hbm,
    user_dual_hbm,
    item_dual_hbm,
    out_users,
    out_items,
    out_user_duals,
    out_item_duals,
    act,
    coords,
    user_owner,
    item_owner,
    slabs,
    time_factor,
    packed,
    landed,
    held,
    khatri,
    gath,
    zsend,
    kbuf,
    gpart,
    xland,
    yland,
    high_part,
    fix,
    fix_land,
    gland,
    gfull,
    base,
    approx,
    partial,
    tland,
    cland,
    dense,
    first_land,
    middle,
    last_land,
    opack,
    oland,
    sems,
    load_sems,
):
    x, y, c, z = (lax.axis_index(name) for name in WIDE_NARROW)
    wide = (x * SIDE + y) * CORES + c
    twin = (x * SIDE + y) * CORES + (1 - c)
    twin_dev = (x, y, 1 - c, z)

    def x_dev(d):
        return (lax.rem(x + d, SIDE), y, c, z)

    def y_dev(d):
        return (x, lax.rem(y + d, SIDE), c, z)

    def z_at(d):
        return lax.rem(z + d, DEPTH)

    def z_dev(d):
        return (x, y, c, z_at(d))

    around = (4, 3, 5, 2, 6, 1, 7)

    barrier = pltpu.get_barrier_semaphore()
    peers = [x_dev(d) for d in (1, 2, 3)] + [y_dev(d) for d in (1, 2, 3)]
    peers += [z_dev(d) for d in range(1, DEPTH)] + [twin_dev]
    for peer in peers:
        pl.semaphore_signal(barrier, inc=1, device_id=peer, device_id_type=MESH)

    moves = (
        (item_factor_hbm, slabs.at[0]),
        (item_dual_hbm, slabs.at[1]),
        (user_factor_hbm, slabs.at[2]),
        (user_dual_hbm, slabs.at[3]),
        (time_factor_hbm, time_factor),
        (coords_hbm, coords),
        (user_owner_hbm, user_owner),
        (item_owner_hbm, item_owner),
        (act_hbm.at[0], act),
    )
    loads = [
        pltpu.make_async_copy(src, dst, load_sems.at[i]) for i, (src, dst) in enumerate(moves)
    ]
    for load in loads:
        load.start()

    groups = []

    class Group:
        def __init__(self, ref):
            k = 2 * len(groups)
            assert k + 1 < SEMS
            groups.append(self)
            self.whole = pltpu.make_async_remote_copy(
                src_ref=ref,
                dst_ref=ref,
                send_sem=sems.at[k],
                recv_sem=sems.at[k + 1],
                device_id=twin_dev,
                device_id_type=MESH,
            )
            self.pair = dict(send_sem=sems.at[k], recv_sem=sems.at[k + 1], device_id_type=MESH)

        def send(self, src, dst, device):
            pltpu.make_async_remote_copy(
                src_ref=src, dst_ref=dst, device_id=device, **self.pair
            ).start()

        def take(self):
            self.whole.wait_recv()

    def pack(which):
        stacked = jnp.concatenate(
            [slabs[which, :, t * 128 : (t + 1) * 128] for t in range(4)], axis=0
        )
        packed[which] = stacked.T

    def lines(place, size):
        return pl.ds(pl.multiple_of(place * size, size), size)

    def unpack(which):
        for t in range(4):
            held[which, t * 16 : (t + 1) * 16] = jnp.concatenate(
                [landed[which, n, :, t * 32 : (t + 1) * 32] for n in range(DEPTH)], axis=1
            )

    loads[0].wait()
    pl.semaphore_wait(barrier, len(peers))

    rows_group = Group(landed.at[:, 0:7])

    def send_rows():
        for load in loads[1:8]:
            load.wait()
        for a in range(4):
            pack(a)
            landed[a, z] = packed[a, lines(z, 16)]
        for d in around:
            rows_group.send(packed.at[:, lines(z_at(d), 16)], landed.at[:, z], z_dev(d))

    def take_rows():
        rows_group.take()
        for a in range(4):
            unpack(a)

    def gather(p, halves, after_start, after_middle, after_plane):
        buf = gath.at[p]
        own = (buf.at[0, c, y, x], buf.at[1, c, x, y])
        for h in range(2):
            own[h][...] = halves[h].astype(BF16)
        starts = Group(buf.at[0, 0, 0:2, 0:3])
        for d in (2, 1, 3):
            for h in range(2):
                starts.send(own[h], own[h], (x_dev, y_dev)[h](d))
        after_start()
        starts.take()
        middles = Group(buf.at[:, 0, 0:3])
        mine = (buf.at[0, c, y], buf.at[1, c, x])
        for d in (2, 1, 3):
            for h in range(2):
                middles.send(mine[h], mine[h], (y_dev, x_dev)[h](d))
        after_middle()
        middles.take()
        twins = Group(buf.at[:, 0])
        for h in range(2):
            twins.send(buf.at[h, c], buf.at[h, c], twin_dev)
        after_plane()
        twins.take()

    def fetch(p, coord, owner):
        def choose(j):
            place = owner[coords[coord, wide * DEPTH + j]]
            a, b, core = place // 8, (place // 2) % SIDE, place % CORES
            zsend[p, j, 0:2] = gath[p, 0, core, b, a].reshape(2, 16, RANK)
            zsend[p, j, 2:4] = gath[p, 1, core, a, b].reshape(2, 16, RANK)

        fetched = Group(kbuf.at[p, 0:7])
        for d in around:
            choose(z_at(d))
            fetched.send(zsend.at[p, z_at(d)], kbuf.at[p, z], z_dev(d))
        choose(z)
        kbuf[p, z] = zsend[p, z]
        return fetched

    def gram_local(p, rows):
        gpart[p, 0:RANK] = exact_dot(rows.T, rows)

    def gram_x(p):
        group = Group(xland.at[p])
        for d in (2, 1, 3):
            group.send(
                gpart.at[p, lines(lax.rem(x + d, SIDE), 64)], xland.at[p, d - 1], x_dev(d)
            )
        return group

    def gram_y(p, group):
        group.take()
        gpart[p, RANK : RANK + 64] = (gpart[p, lines(x, 64)] + xland[p, 0]) + (
            xland[p, 1] + xland[p, 2]
        )
        group = Group(yland.at[p, 0:3])
        for d in (2, 1, 3):
            group.send(
                gpart.at[p, lines(lax.rem(y + d, SIDE) + 16, 16)], yland.at[p, d - 1], y_dev(d)
            )
        return group

    def gram_twin(p, group):
        group.take()
        gpart[p, RANK + 64 : RANK + 80] = (gpart[p, lines(y + 16, 16)] + yland[p, 0]) + (
            yland[p, 1] + yland[p, 2]
        )
        group = Group(yland.at[p, 3])
        group.send(gpart.at[p, RANK + 64 : RANK + 80], yland.at[p, 3], twin_dev)
        return group

    def gram_z(p, group):
        group.take()
        both = gpart[p, RANK + 64 : RANK + 80] + yland[p, 3]
        gpart[p, RANK + 80 : RANK + 88] = jnp.where(c == 0, both[0:8], both[8:16])
        group = Group(gland.at[p, 0:7])
        for d in around:
            group.send(gpart.at[p, RANK + 80 : RANK + 88], gland.at[p, z], z_dev(d))
        gland[p, z] = gpart[p, RANK + 80 : RANK + 88]
        return group

    def fix_local(rows):
        high = rows.astype(BF16)
        low = rows - high.astype(F32)
        missed = lax.dot_general(
            (high.astype(F32) + 0.5 * low).astype(BF16),
            low.astype(BF16),
            (((0,), (0,)), ((), ())),
            preferred_element_type=F32,
        )
        fix[0:RANK] = (missed + missed.T).astype(BF16)

    def fix_x():
        group = Group(fix_land.at[:, 0:64])
        for d in (2, 1, 3):
            group.send(
                fix.at[lines(lax.rem(x + d, SIDE), 64)], fix_land.at[d - 1, 0:64], x_dev(d)
            )
        return group

    def fix_y(group):
        group.take()
        total = fix[lines(x, 64)].astype(F32)
        for d in (1, 2, 3):
            total += fix_land[d - 1, 0:64].astype(F32)
        fix[RANK : RANK + 64] = total.astype(BF16)
        group = Group(fix_land.at[:, 64:80])
        for d in (2, 1, 3):
            group.send(
                fix.at[lines(lax.rem(y + d, SIDE) + 16, 16)], fix_land.at[d - 1, 64:80], y_dev(d)
            )
        return group

    def fix_twin(group):
        group.take()
        total = fix[lines(y + 16, 16)].astype(F32)
        for d in (1, 2, 3):
            total += fix_land[d - 1, 64:80].astype(F32)
        fix[RANK + 64 : RANK + 80] = total.astype(BF16)
        group = Group(fix_land.at[0, 80:96])
        group.send(fix.at[RANK + 64 : RANK + 80], fix_land.at[0, 80:96], twin_dev)
        return group

    def gram_high(p, group):
        total = jnp.zeros((RANK, RANK), F32)
        for h in range(2):
            for a in range(SIDE):
                some = gath[p, h, a // 2, (a % 2) * 2 : (a % 2) * 2 + 2].reshape(256, RANK)
                total += lax.dot_general(
                    some, some, (((0,), (0,)), ((), ())), preferred_element_type=F32
                )
        high_part[...] = total
        group.take()
        own = lines(wide, 8)
        both = fix[RANK + 64 : RANK + 80].astype(F32) + fix_land[0, 80:96].astype(F32)
        high_part[own] += jnp.where(c == 0, both[0:8], both[8:16])
        group = Group(gland.at[p, 0:7])
        for d in around:
            group.send(high_part.at[own], gland.at[p, z], z_dev(d))
        gland[p, z] = high_part[own]
        return group

    def gram_sum(p, group):
        group.take()
        spot = gfull.at[p, c, y, x]
        spot[...] = jnp.sum(gland[p], axis=0)
        group = Group(gfull.at[p, 0, 0, 0:3])
        for d in (2, 1, 3):
            group.send(spot, spot, x_dev(d))
        return group

    def gram_line(p, group):
        group.take()
        line = gfull.at[p, c, y]
        group = Group(gfull.at[p, 0, 0:3])
        for d in (2, 1, 3):
            group.send(line, line, y_dev(d))
        return group

    def gram_plane(p, group):
        group.take()
        plane = gfull.at[p, c]
        group = Group(gfull.at[p, 0])
        group.send(plane, plane, twin_dev)
        return group

    def inverse_start(p, group):
        group.take()
        gram = gfull[p].transpose(2, 1, 0, 3, 4).reshape(RANK, RANK) * time_gram
        penalty = jnp.sum(gram * eye) / RANK
        base[...] = gram / penalty + eye
        t = SCALES[0]
        gain = 2.0 * t * t / (2.0 * t * t - 1.0)
        approx[...] = (eye * 2.0 - base[...] * (1.0 / 129.0)) * (gain / 129.0)
        return penalty

    def split(a):
        high = a.astype(BF16)
        return high, (a - high.astype(F32)).astype(BF16)

    def near_dot(a, b):
        (ah, al), (bh, bl) = split(a), split(b)
        return (
            jnp.dot(ah, bl, preferred_element_type=F32)
            + jnp.dot(al, bh, preferred_element_type=F32)
        ) + jnp.dot(ah, bh, preferred_element_type=F32)

    def inverse_steps(first, last):
        dot = near_dot if last < STEPS else exact_dot

        def step(_, t):
            t2 = 2.0 * t * t - 1.0
            now = approx[...]
            error = eye - dot(base[...], now)
            approx[...] = (now + dot(now, error)) * ((t2 + 1.0) / t2)
            return t2

        lax.fori_loop(first, last, step, F32(SCALES[first + 1]))

    def tile_half(p, h, forward, khatri_t):
        total = jnp.zeros((BLOCK // 2, RANK), F32)
        cut = slice(h * 256, (h + 1) * 256)
        for k in range(TIMES):
            if forward:
                total += jnp.dot(act[k, cut, :], khatri[k], preferred_element_type=F32)
            else:
                total += jnp.dot(khatri_t[k], act[k, :, cut], preferred_element_type=F32)
        if not forward:
            total = total.T
        partial[p, h] = total.reshape(2, DEPTH, 16, RANK).swapaxes(0, 1)
        group = Group(tland.at[p, h, 0:7])
        for d in around:
            group.send(partial.at[p, h, z_at(d)], tland.at[p, h, z], z_dev(d))
        tland[p, h, z] = partial[p, h, z]
        return group

    def reduced(p, coord, owner, arrived, gram):
        targets = [owner[coords[coord, wide * DEPTH + j]] for j in range(DEPTH)]
        twin_targets = [owner[coords[coord, twin * DEPTH + j]] for j in range(DEPTH)]

        def pass_on(h):
            arrived[h].take()
            twins = Group(cland.at[p, h])
            twins.send(tland.at[p, h], cland.at[p, h], twin_dev)
            return twins

        def spread(h, twins):
            twins.take()
            firsts = [Group(first_land.at[p, h, v]) for v in range(2)]
            for d in (2, 1, 3, 0):
                for v in range(2):
                    a = lax.rem((x, y)[v] + d, SIDE)
                    cut = slice(v * 128, (v + 1) * 128)

                    def place(b, carry):
                        block = ((a * SIDE + b) if v == 0 else (b * SIDE + a)) * CORES + c
                        total = jnp.zeros((2, 16, 128), F32)
                        for j in range(DEPTH):
                            total += tland[p, h, j, :, :, cut] * (targets[j] == block).astype(F32)
                            total += cland[p, h, j, :, :, cut] * (
                                twin_targets[j] == block
                            ).astype(F32)
                        dense[p, h, v, a, b] = total
                        return carry

                    lax.fori_loop(0, SIDE, place, 0)
                    if d:
                        firsts[v].send(
                            dense.at[p, h, v, a],
                            first_land.at[p, h, v, d - 1],
                            (x_dev, y_dev)[v](d),
                        )
            return firsts

        def spread_on(h, firsts):
            seconds = [Group(last_land.at[p, h, v]) for v in range(2)]
            for v in range(2):
                firsts[v].take()
                middle[p, h, v] = (dense[p, h, v, (x, y)[v]] + first_land[p, h, v, 0]) + (
                    first_land[p, h, v, 1] + first_land[p, h, v, 2]
                )
                for d in (2, 1, 3):
                    seconds[v].send(
                        middle.at[p, h, v, lax.rem((y, x)[v] + d, SIDE)],
                        last_land.at[p, h, v, d - 1],
                        (y_dev, x_dev)[v](d),
                    )
            return seconds

        def finish(h, seconds):
            parts = []
            for v in range(2):
                seconds[v].take()
                total = (middle[p, h, v, (y, x)[v]] + last_land[p, h, v, 0]) + (
                    last_land[p, h, v, 1] + last_land[p, h, v, 2]
                )
                parts.append(total.reshape(32, 128))
            return jnp.concatenate(parts, axis=1)

        gram = gram_sum(p, gram)
        twins = [pass_on(0)]
        gram = gram_line(p, gram)
        firsts = [spread(0, twins[0])]
        gram = gram_plane(p, gram)
        twins.append(pass_on(1))
        penalty = inverse_start(p, gram)
        inverse_steps(0, 1)
        seconds = [spread_on(0, firsts[0])]
        firsts.append(spread(1, twins[1]))
        inverse_steps(1, 3)
        seconds.append(spread_on(1, firsts[1]))
        inverse_steps(3, 4)
        inverse_steps(4, STEPS)
        return jnp.concatenate([finish(h, seconds[h]) for h in range(2)], axis=0), penalty

    def admm(sums, factor, dual, penalty):
        inverse = approx[...]
        for _ in range(PASSES):
            target = exact_dot(sums + penalty * (factor + dual), inverse) / penalty
            factor = jnp.maximum(target - dual, 0.0)
            dual = dual + factor - target
        return factor, dual

    def give_back(p, factor, dual):
        for a, rows in ((0, factor), (1, dual)):
            for n in range(DEPTH):
                opack[p, n, a] = jnp.concatenate(
                    [
                        rows[t * 16 : (t + 1) * 16, n * 32 : (n + 1) * 32]
                        for t in range(4)
                    ],
                    axis=1,
                )
        group = Group(oland.at[p, :, 0:7])
        for d in around:
            group.send(opack.at[p, z_at(d)], oland.at[p, :, z], z_dev(d))
        oland[p, :, z] = opack[p, z]
        return group

    def take_back(p, group, outs):
        group.take()
        for a in range(2):
            turned = oland[p, a].reshape(128, 128).T
            for t in range(4):
                outs[a][:, t * 128 : (t + 1) * 128] = turned[t * 32 : (t + 1) * 32, :]

    nothing = lambda: None

    def table(p, low):
        if p == 0:
            for k in range(TIMES):
                khatri[k] = (low * times[k : k + 1, :]).astype(BF16)
            return None
        turned = low.T
        columns = times.T
        return [(turned * columns[:, k : k + 1]).astype(BF16) for k in range(TIMES)]

    gather(
        0,
        [slabs[0, :, 0:256], slabs[0, :, 256:512]],
        nothing,
        send_rows,
        nothing,
    )
    fetched = fetch(0, 1, item_owner)
    times = time_factor[...]
    time_gram = exact_dot(times.T, times)
    eye = (
        lax.broadcasted_iota(jnp.int32, (RANK, RANK), 0)
        == lax.broadcasted_iota(jnp.int32, (RANK, RANK), 1)
    ).astype(F32)
    take_rows()
    gram_local(0, held[0])
    gram = gram_twin(0, gram_y(0, gram_x(0)))
    fetched.take()
    loads[8].wait()
    turned = jnp.concatenate(
        [kbuf[0, :, 2 * h : 2 * h + 2].reshape(RANK, 256) for h in range(2)], axis=1
    )
    table(0, turned.astype(F32).T)
    gram = gram_z(0, gram)
    arrived = [tile_half(0, h, True, None) for h in range(2)]
    sums, penalty = reduced(0, 0, user_owner, arrived, gram)
    users, user_duals = admm(sums, held[2], held[3], penalty)

    returned = []
    grams = []
    gather(
        1,
        [users[0:32], users[32:64]],
        lambda: (fix_local(users), grams.append(fix_x())),
        lambda: (
            grams.append(fix_y(grams[0])),
            returned.append(give_back(0, users, user_duals)),
        ),
        lambda: grams.append(fix_twin(grams[1])),
    )
    fetched = fetch(1, 0, user_owner)
    gram = gram_high(1, grams[2])
    take_back(0, returned[0], (out_users, out_user_duals))
    fetched.take()
    khatri_t = table(1, kbuf[1].swapaxes(0, 1).reshape(BLOCK, RANK).astype(F32))
    arrived = [tile_half(1, h, False, khatri_t) for h in range(2)]
    sums, penalty = reduced(1, 1, item_owner, arrived, gram)
    items, item_duals = admm(sums, held[0], held[1], penalty)
    take_back(1, give_back(1, items, item_duals), (out_items, out_item_duals))
    for group in groups:
        group.whole.wait_send()


def settle_kernel(*refs):
    for a in range(4):
        refs[4 + a][...] = refs[a][...]


def local(
    activity,
    tile_coords,
    user_owner,
    item_owner,
    user_factor,
    item_factor,
    time_factor,
    user_dual,
    item_dual,
):
    hbm = pl.BlockSpec(memory_space=pltpu.HBM)
    vmem = pl.BlockSpec(memory_space=pltpu.VMEM)
    slab = jax.ShapeDtypeStruct((RANK // DEPTH, BLOCK), F32)
    outs = pl.pallas_call(
        sweep_kernel,
        out_shape=(slab,) * 4,
        in_specs=[hbm] * 9,
        out_specs=(vmem,) * 4,
        scratch_shapes=[
            pltpu.VMEM((TIMES, BLOCK, BLOCK), BF16),
            pltpu.SMEM((2, RANK), jnp.int32),
            pltpu.SMEM((32,), jnp.int32),
            pltpu.SMEM((32,), jnp.int32),
            pltpu.VMEM((4, RANK // DEPTH, BLOCK), F32),
            pltpu.VMEM((TIMES, RANK), F32),
            pltpu.VMEM((4, 128, 128), F32),
            pltpu.VMEM((4, DEPTH, 16, 128), F32),
            pltpu.VMEM((4, 64, RANK), F32),
            pltpu.VMEM((TIMES, BLOCK, RANK), BF16),
            pltpu.VMEM((2, 2, CORES, SIDE, SIDE, 32, RANK), BF16),
            pltpu.VMEM((2, DEPTH, 4, 16, RANK), BF16),
            pltpu.VMEM((2, DEPTH, 4, 16, RANK), BF16),
            pltpu.VMEM((1, RANK + 88, RANK), F32),
            pltpu.VMEM((1, SIDE - 1, 64, RANK), F32),
            pltpu.VMEM((1, SIDE, 16, RANK), F32),
            pltpu.VMEM((RANK, RANK), F32),
            pltpu.VMEM((RANK + 80, RANK), BF16),
            pltpu.VMEM((SIDE - 1, 96, RANK), BF16),
            pltpu.VMEM((2, DEPTH, 8, RANK), F32),
            pltpu.VMEM((2, CORES, SIDE, SIDE, 8, RANK), F32),
            pltpu.VMEM((RANK, RANK), F32),
            pltpu.VMEM((RANK, RANK), F32),
            pltpu.VMEM((2, 2, DEPTH, 2, 16, RANK), F32),
            pltpu.VMEM((2, 2, DEPTH, 2, 16, RANK), F32),
            pltpu.VMEM((2, 2, DEPTH, 2, 16, RANK), F32),
            pltpu.VMEM((2, 2, 2, SIDE, SIDE, 2, 16, 128), F32),
            pltpu.VMEM((2, 2, 2, SIDE - 1, SIDE, 2, 16, 128), F32),
            pltpu.VMEM((2, 2, 2, SIDE, 2, 16, 128), F32),
            pltpu.VMEM((2, 2, 2, SIDE - 1, 2, 16, 128), F32),
            pltpu.VMEM((2, DEPTH, 2, 16, 128), F32),
            pltpu.VMEM((2, 2, DEPTH, 16, 128), F32),
            pltpu.SemaphoreType.DMA((SEMS,)),
            pltpu.SemaphoreType.DMA((9,)),
        ],
        compiler_params=pltpu.CompilerParams(
            collective_id=0, has_side_effects=True, vmem_limit_bytes=56 * 2**20
        ),
        name="sweep",
    )(
        activity,
        tile_coords.T,
        user_owner,
        item_owner,
        user_factor.T,
        item_factor.T,
        time_factor,
        user_dual.T,
        item_dual.T,
    )
    outs = pl.pallas_call(settle_kernel, out_shape=(slab,) * 4, name="settle")(*outs)
    users, items, user_duals, item_duals = (out.T for out in outs)
    return (users, items, user_duals, item_duals)


def solution(mesh):
    split = Mesh(
        mesh.devices.reshape(SIDE, SIDE, CORES, mesh.shape["narrow"]),
        WIDE_NARROW,
    )
    in_specs = (
        P(WIDE_NARROW, None, None, None),
        P(),
        P(),
        P(),
        P(WIDE, "narrow"),
        P(WIDE, "narrow"),
        P(),
        P(WIDE, "narrow"),
        P(WIDE, "narrow"),
    )
    out_specs = (P(WIDE, "narrow"), P(WIDE, "narrow"), P(WIDE, "narrow"), P(WIDE, "narrow"))
    return jax.shard_map(local, mesh=split, in_specs=in_specs, out_specs=out_specs, check_vma=False)
```

```python
import jax
import jax.numpy as jnp
from jax import lax
from jax.experimental import pallas as pl
from jax.experimental.pallas import tpu as pltpu
from jax.sharding import Mesh
from jax.sharding import PartitionSpec as P

RANK = 256
BLOCK = 512
TIMES = 8
PASSES = 2
SIDE = 4
CORES = 2
DEPTH = 8
STEPS = 6
SCALES = [129.0 / 128.0]
for _ in range(STEPS):
    SCALES.append(2.0 * SCALES[-1] ** 2 - 1.0)
MESH = pl.DeviceIdType.MESH
WIDE = ("wide_0", "wide_1", "wide_2")
WIDE_NARROW = ("wide_0", "wide_1", "wide_2", "narrow")
SEMS = 104
F32 = jnp.float32
BF16 = jnp.bfloat16


def exact_dot(a, b):
    return jnp.dot(a, b, precision=lax.Precision.HIGHEST, preferred_element_type=F32)


def sweep_kernel(
    act_hbm,
    coords_hbm,
    user_owner_hbm,
    item_owner_hbm,
    user_factor_hbm,
    item_factor_hbm,
    time_factor_hbm,
    user_dual_hbm,
    item_dual_hbm,
    out_users,
    out_items,
    out_user_duals,
    out_item_duals,
    act,
    coords,
    user_owner,
    item_owner,
    slabs,
    time_factor,
    packed,
    landed,
    held,
    khatri,
    gath,
    zsend,
    kbuf,
    gpart,
    xland,
    yland,
    high_part,
    fix,
    fix_land,
    gland,
    gfull,
    base,
    approx,
    partial,
    tland,
    cland,
    dense,
    first_land,
    middle,
    last_land,
    opack,
    oland,
    sems,
    load_sems,
):
    x, y, c, z = (lax.axis_index(name) for name in WIDE_NARROW)
    wide = (x * SIDE + y) * CORES + c
    twin = (x * SIDE + y) * CORES + (1 - c)
    twin_dev = (x, y, 1 - c, z)

    def x_dev(d):
        return (lax.rem(x + d, SIDE), y, c, z)

    def y_dev(d):
        return (x, lax.rem(y + d, SIDE), c, z)

    def z_at(d):
        return lax.rem(z + d, DEPTH)

    def z_dev(d):
        return (x, y, c, z_at(d))

    around = (4, 3, 5, 2, 6, 1, 7)

    barrier = pltpu.get_barrier_semaphore()
    peers = [x_dev(d) for d in (1, 2, 3)] + [y_dev(d) for d in (1, 2, 3)]
    peers += [z_dev(d) for d in range(1, DEPTH)] + [twin_dev]
    for peer in peers:
        pl.semaphore_signal(barrier, inc=1, device_id=peer, device_id_type=MESH)

    moves = (
        (item_factor_hbm, slabs.at[0]),
        (item_dual_hbm, slabs.at[1]),
        (user_factor_hbm, slabs.at[2]),
        (user_dual_hbm, slabs.at[3]),
        (time_factor_hbm, time_factor),
        (coords_hbm, coords),
        (user_owner_hbm, user_owner),
        (item_owner_hbm, item_owner),
        (act_hbm.at[0], act),
    )
    loads = [
        pltpu.make_async_copy(src, dst, load_sems.at[i]) for i, (src, dst) in enumerate(moves)
    ]
    for load in loads:
        load.start()

    groups = []

    class Group:
        def __init__(self, ref):
            k = 2 * len(groups)
            assert k + 1 < SEMS
            groups.append(self)
            self.whole = pltpu.make_async_remote_copy(
                src_ref=ref,
                dst_ref=ref,
                send_sem=sems.at[k],
                recv_sem=sems.at[k + 1],
                device_id=twin_dev,
                device_id_type=MESH,
            )
            self.pair = dict(send_sem=sems.at[k], recv_sem=sems.at[k + 1], device_id_type=MESH)

        def send(self, src, dst, device):
            pltpu.make_async_remote_copy(
                src_ref=src, dst_ref=dst, device_id=device, **self.pair
            ).start()

        def take(self):
            self.whole.wait_recv()

    def pack(which):
        stacked = jnp.concatenate(
            [slabs[which, :, t * 128 : (t + 1) * 128] for t in range(4)], axis=0
        )
        packed[which] = stacked.T

    def lines(place, size):
        return pl.ds(pl.multiple_of(place * size, size), size)

    def unpack(which):
        for t in range(4):
            held[which, t * 16 : (t + 1) * 16] = jnp.concatenate(
                [landed[which, n, :, t * 32 : (t + 1) * 32] for n in range(DEPTH)], axis=1
            )

    loads[0].wait()
    pl.semaphore_wait(barrier, len(peers))

    rows_group = Group(landed.at[:, 0:7])

    def send_rows():
        for load in loads[1:8]:
            load.wait()
        for a in range(4):
            pack(a)
            landed[a, z] = packed[a, lines(z, 16)]
        for d in around:
            rows_group.send(packed.at[:, lines(z_at(d), 16)], landed.at[:, z], z_dev(d))

    def take_rows():
        rows_group.take()
        unpack(0)

    def gather(p, halves, after_start, after_middle, after_plane):
        buf = gath.at[p]
        own = (buf.at[0, c, y, x], buf.at[1, c, x, y])
        for h in range(2):
            own[h][...] = halves[h].astype(BF16)
        starts = Group(buf.at[0, 0, 0:2, 0:3])
        for d in (2, 1, 3):
            for h in range(2):
                starts.send(own[h], own[h], (x_dev, y_dev)[h](d))
        after_start()
        starts.take()
        middles = Group(buf.at[:, 0, 0:3])
        mine = (buf.at[0, c, y], buf.at[1, c, x])
        for d in (2, 1, 3):
            for h in range(2):
                middles.send(mine[h], mine[h], (y_dev, x_dev)[h](d))
        after_middle()
        middles.take()
        twins = Group(buf.at[:, 0])
        for h in range(2):
            twins.send(buf.at[h, c], buf.at[h, c], twin_dev)
        after_plane()
        twins.take()

    def fetch(p, coord, owner):
        def choose(j):
            place = owner[coords[coord, wide * DEPTH + j]]
            a, b, core = place // 8, (place // 2) % SIDE, place % CORES
            zsend[p, j, 0:2] = gath[p, 0, core, b, a].reshape(2, 16, RANK)
            zsend[p, j, 2:4] = gath[p, 1, core, a, b].reshape(2, 16, RANK)

        fetched = Group(kbuf.at[p, 0:7])
        for d in around:
            choose(z_at(d))
            fetched.send(zsend.at[p, z_at(d)], kbuf.at[p, z], z_dev(d))
        choose(z)
        kbuf[p, z] = zsend[p, z]
        return fetched

    def gram_local(p, rows):
        gpart[p, 0:RANK] = exact_dot(rows.T, rows)

    def gram_x(p):
        group = Group(xland.at[p])
        for d in (2, 1, 3):
            group.send(
                gpart.at[p, lines(lax.rem(x + d, SIDE), 64)], xland.at[p, d - 1], x_dev(d)
            )
        return group

    def gram_y(p, group):
        group.take()
        gpart[p, RANK : RANK + 64] = (gpart[p, lines(x, 64)] + xland[p, 0]) + (
            xland[p, 1] + xland[p, 2]
        )
        group = Group(yland.at[p, 0:3])
        for d in (2, 1, 3):
            group.send(
                gpart.at[p, lines(lax.rem(y + d, SIDE) + 16, 16)], yland.at[p, d - 1], y_dev(d)
            )
        return group

    def gram_twin(p, group):
        group.take()
        gpart[p, RANK + 64 : RANK + 80] = (gpart[p, lines(y + 16, 16)] + yland[p, 0]) + (
            yland[p, 1] + yland[p, 2]
        )
        group = Group(yland.at[p, 3])
        group.send(gpart.at[p, RANK + 64 : RANK + 80], yland.at[p, 3], twin_dev)
        return group

    def gram_z(p, group):
        group.take()
        both = gpart[p, RANK + 64 : RANK + 80] + yland[p, 3]
        gpart[p, RANK + 80 : RANK + 88] = jnp.where(c == 0, both[0:8], both[8:16])
        group = Group(gland.at[p, 0:7])
        for d in around:
            group.send(gpart.at[p, RANK + 80 : RANK + 88], gland.at[p, z], z_dev(d))
        gland[p, z] = gpart[p, RANK + 80 : RANK + 88]
        return group

    def fix_local(rows):
        high = rows.astype(BF16)
        low = rows - high.astype(F32)
        missed = lax.dot_general(
            (high.astype(F32) + 0.5 * low).astype(BF16),
            low.astype(BF16),
            (((0,), (0,)), ((), ())),
            preferred_element_type=F32,
        )
        fix[0:RANK] = (missed + missed.T).astype(BF16)

    def fix_x():
        group = Group(fix_land.at[:, 0:64])
        for d in (2, 1, 3):
            group.send(
                fix.at[lines(lax.rem(x + d, SIDE), 64)], fix_land.at[d - 1, 0:64], x_dev(d)
            )
        return group

    def fix_y(group):
        group.take()
        total = fix[lines(x, 64)].astype(F32)
        for d in (1, 2, 3):
            total += fix_land[d - 1, 0:64].astype(F32)
        fix[RANK : RANK + 64] = total.astype(BF16)
        group = Group(fix_land.at[:, 64:80])
        for d in (2, 1, 3):
            group.send(
                fix.at[lines(lax.rem(y + d, SIDE) + 16, 16)], fix_land.at[d - 1, 64:80], y_dev(d)
            )
        return group

    def fix_twin(group):
        group.take()
        total = fix[lines(y + 16, 16)].astype(F32)
        for d in (1, 2, 3):
            total += fix_land[d - 1, 64:80].astype(F32)
        fix[RANK + 64 : RANK + 80] = total.astype(BF16)
        group = Group(fix_land.at[0, 80:96])
        group.send(fix.at[RANK + 64 : RANK + 80], fix_land.at[0, 80:96], twin_dev)
        return group

    def gram_high(p, group):
        total = jnp.zeros((RANK, RANK), F32)
        for h in range(2):
            for a in range(SIDE):
                some = gath[p, h, a // 2, (a % 2) * 2 : (a % 2) * 2 + 2].reshape(256, RANK)
                total += lax.dot_general(
                    some, some, (((0,), (0,)), ((), ())), preferred_element_type=F32
                )
        high_part[...] = total
        group.take()
        own = lines(wide, 8)
        both = fix[RANK + 64 : RANK + 80].astype(F32) + fix_land[0, 80:96].astype(F32)
        high_part[own] += jnp.where(c == 0, both[0:8], both[8:16])
        group = Group(gland.at[p, 0:7])
        for d in around:
            group.send(high_part.at[own], gland.at[p, z], z_dev(d))
        gland[p, z] = high_part[own]
        return group

    def gram_sum(p, group):
        group.take()
        spot = gfull.at[p, c, y, x]
        spot[...] = jnp.sum(gland[p], axis=0)
        group = Group(gfull.at[p, 0, 0, 0:3])
        for d in (2, 1, 3):
            group.send(spot, spot, x_dev(d))
        return group

    def gram_line(p, group):
        group.take()
        line = gfull.at[p, c, y]
        group = Group(gfull.at[p, 0, 0:3])
        for d in (2, 1, 3):
            group.send(line, line, y_dev(d))
        return group

    def gram_plane(p, group):
        group.take()
        plane = gfull.at[p, c]
        group = Group(gfull.at[p, 0])
        group.send(plane, plane, twin_dev)
        return group

    def inverse_start(p, group):
        group.take()
        gram = gfull[p].transpose(2, 1, 0, 3, 4).reshape(RANK, RANK) * time_gram
        penalty = jnp.sum(gram * eye) / RANK
        base[...] = gram / penalty + eye
        t = SCALES[0]
        gain = 2.0 * t * t / (2.0 * t * t - 1.0)
        approx[...] = (eye * 2.0 - base[...] * (1.0 / 129.0)) * (gain / 129.0)
        return penalty

    def split(a):
        high = a.astype(BF16)
        return high, (a - high.astype(F32)).astype(BF16)

    def near_dot(a, b):
        (ah, al), (bh, bl) = split(a), split(b)
        return (
            jnp.dot(ah, bl, preferred_element_type=F32)
            + jnp.dot(al, bh, preferred_element_type=F32)
        ) + jnp.dot(ah, bh, preferred_element_type=F32)

    def inverse_steps(first, last):
        dot = near_dot if last < STEPS else exact_dot

        def step(_, t):
            t2 = 2.0 * t * t - 1.0
            now = approx[...]
            error = eye - dot(base[...], now)
            approx[...] = (now + dot(now, error)) * ((t2 + 1.0) / t2)
            return t2

        lax.fori_loop(first, last, step, F32(SCALES[first + 1]))

    def tile_half(p, h, forward, khatri_t):
        total = jnp.zeros((BLOCK // 2, RANK), F32)
        cut = slice(h * 256, (h + 1) * 256)
        for k in range(TIMES):
            if forward:
                total += jnp.dot(act[k, cut, :], khatri[k], preferred_element_type=F32)
            else:
                total += jnp.dot(khatri_t[k], act[k, :, cut], preferred_element_type=F32)
        if not forward:
            total = total.T
        partial[p, h] = total.reshape(2, DEPTH, 16, RANK).swapaxes(0, 1)
        group = Group(tland.at[p, h, 0:7])
        for d in around:
            group.send(partial.at[p, h, z_at(d)], tland.at[p, h, z], z_dev(d))
        tland[p, h, z] = partial[p, h, z]
        return group

    def reduced(p, coord, owner, arrived, gram):
        targets = [owner[coords[coord, wide * DEPTH + j]] for j in range(DEPTH)]
        twin_targets = [owner[coords[coord, twin * DEPTH + j]] for j in range(DEPTH)]

        def pass_on(h):
            arrived[h].take()
            twins = Group(cland.at[p, h])
            twins.send(tland.at[p, h], cland.at[p, h], twin_dev)
            return twins

        def spread(h, twins):
            twins.take()
            firsts = [Group(first_land.at[p, h, v]) for v in range(2)]
            for d in (2, 1, 3, 0):
                for v in range(2):
                    a = lax.rem((x, y)[v] + d, SIDE)
                    cut = slice(v * 128, (v + 1) * 128)

                    def place(b, carry):
                        block = ((a * SIDE + b) if v == 0 else (b * SIDE + a)) * CORES + c
                        total = jnp.zeros((2, 16, 128), F32)
                        for j in range(DEPTH):
                            total += tland[p, h, j, :, :, cut] * (targets[j] == block).astype(F32)
                            total += cland[p, h, j, :, :, cut] * (
                                twin_targets[j] == block
                            ).astype(F32)
                        dense[p, h, v, a, b] = total
                        return carry

                    lax.fori_loop(0, SIDE, place, 0)
                    if d:
                        firsts[v].send(
                            dense.at[p, h, v, a],
                            first_land.at[p, h, v, d - 1],
                            (x_dev, y_dev)[v](d),
                        )
            return firsts

        def spread_on(h, firsts):
            seconds = [Group(last_land.at[p, h, v]) for v in range(2)]
            for v in range(2):
                firsts[v].take()
                middle[p, h, v] = (dense[p, h, v, (x, y)[v]] + first_land[p, h, v, 0]) + (
                    first_land[p, h, v, 1] + first_land[p, h, v, 2]
                )
                for d in (2, 1, 3):
                    seconds[v].send(
                        middle.at[p, h, v, lax.rem((y, x)[v] + d, SIDE)],
                        last_land.at[p, h, v, d - 1],
                        (y_dev, x_dev)[v](d),
                    )
            return seconds

        def finish(h, seconds):
            parts = []
            for v in range(2):
                seconds[v].take()
                total = (middle[p, h, v, (y, x)[v]] + last_land[p, h, v, 0]) + (
                    last_land[p, h, v, 1] + last_land[p, h, v, 2]
                )
                parts.append(total.reshape(32, 128))
            return jnp.concatenate(parts, axis=1)

        gram = gram_sum(p, gram)
        twins = [pass_on(0)]
        gram = gram_line(p, gram)
        firsts = [spread(0, twins[0])]
        gram = gram_plane(p, gram)
        twins.append(pass_on(1))
        penalty = inverse_start(p, gram)
        inverse_steps(0, 1)
        seconds = [spread_on(0, firsts[0])]
        firsts.append(spread(1, twins[1]))
        inverse_steps(1, 3)
        seconds.append(spread_on(1, firsts[1]))
        inverse_steps(3, 4)
        inverse_steps(4, STEPS)
        return jnp.concatenate([finish(h, seconds[h]) for h in range(2)], axis=0), penalty

    def admm(sums, factor, dual, penalty):
        inverse = approx[...]
        for _ in range(PASSES):
            target = exact_dot(sums + penalty * (factor + dual), inverse) / penalty
            factor = jnp.maximum(target - dual, 0.0)
            dual = dual + factor - target
        return factor, dual

    def give_back(p, factor, dual):
        for a, rows in ((0, factor), (1, dual)):
            for n in range(DEPTH):
                opack[p, n, a] = jnp.concatenate(
                    [
                        rows[t * 16 : (t + 1) * 16, n * 32 : (n + 1) * 32]
                        for t in range(4)
                    ],
                    axis=1,
                )
        group = Group(oland.at[p, :, 0:7])
        for d in around:
            group.send(opack.at[p, z_at(d)], oland.at[p, :, z], z_dev(d))
        oland[p, :, z] = opack[p, z]
        return group

    def take_back(p, group, outs):
        group.take()
        for a in range(2):
            turned = oland[p, a].reshape(128, 128).T
            for t in range(4):
                outs[a][:, t * 128 : (t + 1) * 128] = turned[t * 32 : (t + 1) * 32, :]

    nothing = lambda: None

    def table(p, low):
        if p == 0:
            for k in range(TIMES):
                khatri[k] = (low * times[k : k + 1, :]).astype(BF16)
            return None
        turned = low.T
        columns = times.T
        return [(turned * columns[:, k : k + 1]).astype(BF16) for k in range(TIMES)]

    gather(
        0,
        [slabs[0, :, 0:256], slabs[0, :, 256:512]],
        nothing,
        send_rows,
        nothing,
    )
    fetched = fetch(0, 1, item_owner)
    times = time_factor[...]
    time_gram = exact_dot(times.T, times)
    eye = (
        lax.broadcasted_iota(jnp.int32, (RANK, RANK), 0)
        == lax.broadcasted_iota(jnp.int32, (RANK, RANK), 1)
    ).astype(F32)
    take_rows()
    gram_local(0, held[0])
    gram = gram_x(0)
    for a in (1, 2, 3):
        unpack(a)
    gram = gram_twin(0, gram_y(0, gram))
    fetched.take()
    loads[8].wait()
    turned = jnp.concatenate(
        [kbuf[0, :, 2 * h : 2 * h + 2].reshape(RANK, 256) for h in range(2)], axis=1
    )
    table(0, turned.astype(F32).T)
    gram = gram_z(0, gram)
    arrived = [tile_half(0, h, True, None) for h in range(2)]
    sums, penalty = reduced(0, 0, user_owner, arrived, gram)
    users, user_duals = admm(sums, held[2], held[3], penalty)

    returned = []
    grams = []
    gather(
        1,
        [users[0:32], users[32:64]],
        lambda: (fix_local(users), grams.append(fix_x())),
        lambda: (
            grams.append(fix_y(grams[0])),
            returned.append(give_back(0, users, user_duals)),
        ),
        lambda: grams.append(fix_twin(grams[1])),
    )
    fetched = fetch(1, 0, user_owner)
    gram = gram_high(1, grams[2])
    take_back(0, returned[0], (out_users, out_user_duals))
    fetched.take()
    khatri_t = table(1, kbuf[1].swapaxes(0, 1).reshape(BLOCK, RANK).astype(F32))
    arrived = [tile_half(1, h, False, khatri_t) for h in range(2)]
    sums, penalty = reduced(1, 1, item_owner, arrived, gram)
    items, item_duals = admm(sums, held[0], held[1], penalty)
    take_back(1, give_back(1, items, item_duals), (out_items, out_item_duals))
    for group in groups:
        group.whole.wait_send()


def settle_kernel(*refs):
    for a in range(4):
        refs[4 + a][...] = refs[a][...]


def local(
    activity,
    tile_coords,
    user_owner,
    item_owner,
    user_factor,
    item_factor,
    time_factor,
    user_dual,
    item_dual,
):
    hbm = pl.BlockSpec(memory_space=pltpu.HBM)
    vmem = pl.BlockSpec(memory_space=pltpu.VMEM)
    slab = jax.ShapeDtypeStruct((RANK // DEPTH, BLOCK), F32)
    outs = pl.pallas_call(
        sweep_kernel,
        out_shape=(slab,) * 4,
        in_specs=[hbm] * 9,
        out_specs=(vmem,) * 4,
        scratch_shapes=[
            pltpu.VMEM((TIMES, BLOCK, BLOCK), BF16),
            pltpu.SMEM((2, RANK), jnp.int32),
            pltpu.SMEM((32,), jnp.int32),
            pltpu.SMEM((32,), jnp.int32),
            pltpu.VMEM((4, RANK // DEPTH, BLOCK), F32),
            pltpu.VMEM((TIMES, RANK), F32),
            pltpu.VMEM((4, 128, 128), F32),
            pltpu.VMEM((4, DEPTH, 16, 128), F32),
            pltpu.VMEM((4, 64, RANK), F32),
            pltpu.VMEM((TIMES, BLOCK, RANK), BF16),
            pltpu.VMEM((2, 2, CORES, SIDE, SIDE, 32, RANK), BF16),
            pltpu.VMEM((2, DEPTH, 4, 16, RANK), BF16),
            pltpu.VMEM((2, DEPTH, 4, 16, RANK), BF16),
            pltpu.VMEM((1, RANK + 88, RANK), F32),
            pltpu.VMEM((1, SIDE - 1, 64, RANK), F32),
            pltpu.VMEM((1, SIDE, 16, RANK), F32),
            pltpu.VMEM((RANK, RANK), F32),
            pltpu.VMEM((RANK + 80, RANK), BF16),
            pltpu.VMEM((SIDE - 1, 96, RANK), BF16),
            pltpu.VMEM((2, DEPTH, 8, RANK), F32),
            pltpu.VMEM((2, CORES, SIDE, SIDE, 8, RANK), F32),
            pltpu.VMEM((RANK, RANK), F32),
            pltpu.VMEM((RANK, RANK), F32),
            pltpu.VMEM((2, 2, DEPTH, 2, 16, RANK), F32),
            pltpu.VMEM((2, 2, DEPTH, 2, 16, RANK), F32),
            pltpu.VMEM((2, 2, DEPTH, 2, 16, RANK), F32),
            pltpu.VMEM((2, 2, 2, SIDE, SIDE, 2, 16, 128), F32),
            pltpu.VMEM((2, 2, 2, SIDE - 1, SIDE, 2, 16, 128), F32),
            pltpu.VMEM((2, 2, 2, SIDE, 2, 16, 128), F32),
            pltpu.VMEM((2, 2, 2, SIDE - 1, 2, 16, 128), F32),
            pltpu.VMEM((2, DEPTH, 2, 16, 128), F32),
            pltpu.VMEM((2, 2, DEPTH, 16, 128), F32),
            pltpu.SemaphoreType.DMA((SEMS,)),
            pltpu.SemaphoreType.DMA((9,)),
        ],
        compiler_params=pltpu.CompilerParams(
            collective_id=0, has_side_effects=True, vmem_limit_bytes=56 * 2**20
        ),
        name="sweep",
    )(
        activity,
        tile_coords.T,
        user_owner,
        item_owner,
        user_factor.T,
        item_factor.T,
        time_factor,
        user_dual.T,
        item_dual.T,
    )
    outs = pl.pallas_call(settle_kernel, out_shape=(slab,) * 4, name="settle")(*outs)
    users, items, user_duals, item_duals = (out.T for out in outs)
    return (users, items, user_duals, item_duals)


def solution(mesh):
    split = Mesh(
        mesh.devices.reshape(SIDE, SIDE, CORES, mesh.shape["narrow"]),
        WIDE_NARROW,
    )
    in_specs = (
        P(WIDE_NARROW, None, None, None),
        P(),
        P(),
        P(),
        P(WIDE, "narrow"),
        P(WIDE, "narrow"),
        P(),
        P(WIDE, "narrow"),
        P(WIDE, "narrow"),
    )
    out_specs = (P(WIDE, "narrow"), P(WIDE, "narrow"), P(WIDE, "narrow"), P(WIDE, "narrow"))
    return jax.shard_map(local, mesh=split, in_specs=in_specs, out_specs=out_specs, check_vma=False)
```
